256 devices in a mesh: gx: 32 (over y, x, core), gy: 8 (over z).
Axes of the slice: x: 4, y: 4, z: 8, core: 2. Of those that a mesh axis runs over, the one named last changes fastest.
Arguments:
- initial_guess: float32 [16, 512, 16384], P(None, 'gx', 'gy')
- conductivity: float32 [512, 16384], P('gx', 'gy'), may hold values from 0.05 to 0.5
- electrodes: int32 [16], replicated, may hold values from 0 to 8388607
Outputs:
- basis: float32 [48, 512, 16384], P(None, 'gx', 'gy')
- triangle: float32 [48, 48], replicated
The draws below stay inside these ranges and needn't reach their ends.
Inputs may be any that keep to these rules, and one draw needn't show every extreme that they name: `electrodes`: each entry is a flattened cell index (x * 256 + y) * 64 + z.
All inputs are finite; a program needn't handle non-finite values.
Results may differ from the reference program's by a relative error of at most 0.0003.
Values sent between devices are 32-bit elements; how exact they have to be, the bound alone decides.
A program may use at most 128 MiB of HBM per device.

```python
import math
import jax
import jax.numpy as jnp
from jax import lax

SRC = 16
COLS = 48
NZ = 64
NX = 512
NY = 256


def draw_initial_guess(key, part):
    key = jax.random.fold_in(key, 1)
    keys = jax.random.split(key, 3)
    rise_x = 1.0 + 2.0 * jnp.arange(NX, dtype=jnp.float32) / (NX - 1)
    rise_y = 1.0 + 2.0 * jnp.arange(NY, dtype=jnp.float32) / (NY - 1)
    rise = rise_x[:, None, None] * rise_y[None, :, None]
    cell_scale = jnp.exp(jax.random.uniform(keys[1], (NX, NY, NZ), jnp.float32) * math.log(10.0))
    column_scale = jnp.exp(jax.random.uniform(keys[2], (SRC,), jnp.float32) * math.log(10.0))
    root_cells = math.sqrt(NX * NY * NZ)
    values = jax.random.normal(keys[0], (SRC, NX, NY, NZ), jnp.float32)
    factor = 0.3 / root_cells
    grid = factor * values * (rise * cell_scale)[None] * column_scale[:, None, None, None]
    return grid.reshape(SRC, NX, NY * NZ).astype(jnp.float32)


def with_ends(array, own_key, smallest, largest):
    longest = array.shape.index(max(array.shape))
    spots = []
    for shift in (0, 1):
        where = [jax.random.randint(jax.random.fold_in(own_key, axis), (), 0, length) for axis, length in enumerate(array.shape)]
        where[longest] = (where[longest] + shift) % array.shape[longest]
        spots.append(tuple(where))
    return array.at[spots[0]].set(smallest).at[spots[1]].set(largest)


def block_levels(own_key, shape, cuts, least, largest):
    factor_of = 1.0
    for position, parts in cuts:
        draws = jax.random.uniform(jax.random.fold_in(jax.random.fold_in(own_key, 6), position), (parts,), jnp.float32, least / len(cuts), largest / len(cuts))
        factor_of = factor_of * jnp.repeat(jnp.exp(draws), shape[position] // parts).reshape((-1,) + (1,) * (len(shape) - 1 - position))
    return factor_of


def setup_inputs(seed: int = 0) -> dict:
    key_list = jax.random.split(jax.random.key(seed), 4)
    initial_guess = draw_initial_guess(jax.random.fold_in(key_list[3], 71), 0)
    conductivity = jnp.clip(jnp.exp(math.log(0.5) - 2.3025851 * jax.random.uniform(key_list[1], (NX, NY * NZ), jnp.float32) ** block_levels(key_list[1], (NX, NY * NZ), ((0, 32), (1, 8)), -0.2, 0.2)), 0.05, 0.5)
    electrodes = with_ends(jax.random.randint(key_list[2], (SRC,), 0, NX * NY * NZ), jax.random.fold_in(key_list[2], 1), 0, (NX * NY * NZ) - 1).astype(jnp.int32)
    return {"initial_guess": initial_guess, "conductivity": conductivity, "electrodes": electrodes}


NEIGHBOURS = ((2, 1, 1), (0, 1, 1), (1, 2, 1), (1, 0, 1), (1, 1, 2), (1, 1, 0))

def window(values, starts):
    base = values.ndim - 3
    result = values
    for offset, anchor in enumerate(starts):
        axis_number = base + offset
        extent = values.shape[axis_number]
        result = lax.slice_in_dim(result, anchor, anchor + extent - 2, axis=axis_number)
    return result

def stencil(padded_field, padded_cond):
    centre = padded_field[:, 1:-1, 1:-1, 1:-1]
    cond_centre = padded_cond[1:-1, 1:-1, 1:-1]
    total = jnp.zeros_like(centre)
    for starts in NEIGHBOURS:
        coupling = 0.5 * (cond_centre + window(padded_cond, starts))
        total = total + coupling * (centre - window(padded_field, starts))
    return total

def operate(field, conductivity):
    padded_field = jnp.pad(field, ((0, 0), (1, 1), (1, 1), (1, 1)))
    padded_cond = jnp.pad(conductivity, 1)
    return stencil(padded_field, padded_cond)

def reference(initial_guess, conductivity, electrodes):
    cells = NX * NY * NZ
    guess_grid = initial_guess.reshape(SRC, NX, NY, NZ)
    cond_grid = conductivity.reshape(NX, NY, NZ)
    flat_index = jnp.arange(cells, dtype=jnp.int32).reshape(NX, NY, NZ)
    hits = flat_index[None] == electrodes[:, None, None, None]
    source_field = 20.0 * hits.astype(jnp.float32)
    first = source_field - operate(guess_grid, cond_grid)
    second = operate(first, cond_grid) - 0.8 * first
    third = operate(second, cond_grid) - 1.6 * second
    columns = jnp.concatenate([first, second, third], 0).reshape(COLS, cells)
    gram = jnp.dot(columns, columns.T, precision=lax.Precision.HIGHEST)
    lower = jnp.linalg.cholesky(gram)
    scale = math.sqrt(cells)
    solved = jax.scipy.linalg.solve_triangular(lower, columns, lower=True)
    basis = (solved * scale).reshape(COLS, NX, NY * NZ)
    triangle = lower.T / scale
    return (basis, triangle)
```

```python
import functools
import math

import jax
import jax.numpy as jnp
from jax import lax
from jax.experimental import pallas as pl
from jax.experimental.pallas import tpu as pltpu
from jax.sharding import PartitionSpec as P

MESH = pl.DeviceIdType.MESH
NZ = 64
LANES = 128
HALF = 64
SRC = 16
COLS = 48
CX = 16
TILES = 16
REACH = 3
EXT_X = CX + 2 * REACH
EXT_T = TILES + 2
EXT = EXT_T * LANES
MERGED = TILES * LANES
GX, GY = 32, 8
MOVES = ((1, 0), (-1, 0), (0, 1), (0, -1), (1, 1), (1, -1), (-1, 1), (-1, -1))


def tile(t):
    if isinstance(t, int):
        return pl.ds(t * LANES, LANES)
    return pl.ds(pl.multiple_of(t * LANES, LANES), LANES)


def swap_halves(v):
    return pltpu.roll(v, HALF, 1)


def partner(kind, gx, gy, step):
    if kind == 0:
        base = (gx // 8) * 8
        return (base + lax.rem(gx - base + step, 8), gy)
    if kind == 1:
        return (lax.rem(gx + 8 * step, GX), gy)
    return (gx, lax.rem(gy + step, GY))


def place(kind, gx, gy):
    return (lax.rem(gx, 8), gx // 8, gy)[kind]


GROUPS = (8, 4, 8)


def krylov_kernel(
    guess,
    cond,
    electrodes,
    cols,
    gram,
    natural,
    start,
    field,
    cond_ext,
    coef,
    third_out,
    third_in,
    split,
    part0,
    part1,
    part2,
    guess_sem,
    local_sem,
    cond_send,
    cond_recv,
    send,
    recv,
    third_send_sem,
    third_recv_sem,
    sum_send,
    sum_recv,
):
    gx, gy = lax.axis_index("gx"), lax.axis_index("gy")
    f32 = jnp.float32

    def beside(move):
        dx, dy = move
        return (lax.rem(gx + dx + GX, GX), lax.rem(gy + dy + GY, GY))

    loads = [
        pltpu.make_async_copy(guess.at[:, tile(t)], natural.at[t], guess_sem.at[t])
        for t in range(TILES)
    ]
    for load in loads:
        load.start()
    load_cond = pltpu.make_async_copy(
        cond, cond_ext.at[pl.ds(8, CX), pl.ds(2 * LANES, MERGED)], local_sem.at[1]
    )
    load_cond.start()

    barrier = pltpu.get_barrier_semaphore()
    for move in MOVES:
        pl.semaphore_signal(barrier, inc=1, device_id=beside(move), device_id_type=MESH)
    for kind, size in enumerate(GROUPS):
        for step in range(1, size):
            pl.semaphore_signal(
                barrier, inc=1, device_id=partner(kind, gx, gy, step), device_id_type=MESH
            )

    for x in (0, EXT_X - 1):
        for t in (0, EXT_T - 1):
            start[x, :, tile(t)] = jnp.zeros((SRC, LANES), f32)
    for x in (0, 8 + CX):
        for t in (0, EXT_T + 1):
            cond_ext[pl.ds(x, 8), tile(t)] = jnp.zeros((8, LANES), f32)

    for load in loads:
        load.wait()

    def lay_out(x, carry):
        for t in range(TILES):
            start[x + REACH, :, tile(t + 1)] = natural[t, pl.ds(x, SRC, stride=CX), :]
        return carry

    lax.fori_loop(0, CX, lay_out, 0)

    lane = lax.broadcasted_iota(jnp.int32, (SRC, LANES), 1)
    low = lane < HALF

    def pack_third(x, carry):
        near, far = REACH + x, REACH + CX // 2 + x
        third_out[0, x] = jnp.where(
            low, swap_halves(start[near, :, tile(TILES - 1)]), start[far, :, tile(TILES - 1)]
        )
        third_out[1, x] = jnp.where(
            low, start[far, :, tile(2)], swap_halves(start[near, :, tile(2)])
        )
        return carry

    lax.fori_loop(0, CX // 2, pack_third, 0)

    pl.semaphore_wait(barrier, len(MOVES) + sum(GROUPS) - len(GROUPS))

    cond_copies = []
    for i, (dx, dy) in enumerate(MOVES):
        if dx == 0:
            rows_from, rows_to, rows = pl.ds(0, CX), pl.ds(8, CX), CX
        elif dx > 0:
            rows_from, rows_to = pl.ds(CX - 8, 8), pl.ds(0, 8)
        else:
            rows_from, rows_to = pl.ds(0, 8), pl.ds(8 + CX, 8)
        if dy == 0:
            lanes_from, lanes_to = pl.ds(0, MERGED), pl.ds(2 * LANES, MERGED)
        elif dx == 0:
            lanes_from = pl.ds(MERGED - 2 * LANES if dy > 0 else 0, 2 * LANES)
            lanes_to = pl.ds(0 if dy > 0 else (TILES + 2) * LANES, 2 * LANES)
        else:
            lanes_from = tile(TILES - 1 if dy > 0 else 0)
            lanes_to = tile(1 if dy > 0 else TILES + 2)
        cond_copies.append(
            pltpu.make_async_remote_copy(
                src_ref=cond.at[rows_from, lanes_from],
                dst_ref=cond_ext.at[rows_to, lanes_to],
                send_sem=cond_send.at[i],
                recv_sem=cond_recv.at[i],
                device_id=beside((dx, dy)),
                device_id_type=MESH,
            )
        )
    copies = []
    for i, (dx, dy) in enumerate(MOVES):
        depth = REACH if dy == 0 else 2
        if dx == 0:
            x_from, x_to = pl.ds(REACH, CX), pl.ds(REACH, CX)
        elif dx > 0:
            x_from, x_to = pl.ds(REACH + CX - depth, depth), pl.ds(REACH - depth, depth)
        else:
            x_from, x_to = pl.ds(REACH, depth), pl.ds(REACH + CX, depth)
        if dy == 0:
            lanes_from = lanes_to = pl.ds(LANES, MERGED)
        else:
            lanes_from = tile(TILES if dy > 0 else 1)
            lanes_to = tile(0 if dy > 0 else TILES + 1)
        copies.append(
            pltpu.make_async_remote_copy(
                src_ref=start.at[x_from, :, lanes_from],
                dst_ref=start.at[x_to, :, lanes_to],
                send_sem=send.at[i],
                recv_sem=recv.at[i],
                device_id=beside((dx, dy)),
                device_id_type=MESH,
            )
        )
    thirds = [
        pltpu.make_async_remote_copy(
            src_ref=third_out.at[i],
            dst_ref=third_in.at[i],
            send_sem=third_send_sem.at[i],
            recv_sem=third_recv_sem.at[i],
            device_id=beside(move),
            device_id_type=MESH,
        )
        for i, move in enumerate(((0, 1), (0, -1)))
    ]
    for copy in cond_copies + copies + thirds:
        copy.start()

    load_cond.wait()
    for copy in cond_copies:
        copy.wait_recv()
    row = lax.broadcasted_iota(jnp.int32, (CX + 16, LANES), 0)
    lane_c = lax.broadcasted_iota(jnp.int32, (CX + 16, LANES), 1)
    first_x, last_x = gx == 0, gx == GX - 1
    row_from = jnp.where(first_x, 8, 0)
    row_to = jnp.where(last_x, 8 + CX, 16 + CX)
    inside_x = (row >= row_from) & (row < row_to)
    tile_from = jnp.where(gy == 0, 2, 0)
    tile_to = jnp.where(gy == GY - 1, TILES + 2, TILES + 4)
    z = lax.rem(lane_c, HALF)
    low_c = lane_c < HALF

    def couplings(t, carry):
        def load(place):
            row_end = jnp.where((place >= tile_from) & (place < tile_to), row_to, 0)
            return jnp.where(inside_x & (row < row_end), cond_ext[:, tile(place)], 0.0)

        here = load(t + 1)
        below, above = load(t), load(t + 2)
        swapped = swap_halves(here)
        outer = jnp.where(low_c, swap_halves(below), swap_halves(above))
        z_down = jnp.where(z == 0, 0.0, pltpu.roll(here, 1, 1))
        z_up = jnp.where(z == HALF - 1, 0.0, pltpu.roll(here, LANES - 1, 1))
        x_down = pltpu.roll(here, 1, 0)
        x_up = pltpu.roll(here, CX + 15, 0)
        total = 6.0 * here
        for k, there in enumerate((x_down, x_up, swapped, outer, z_down, z_up)):
            total = total + there
            face = jnp.where((here > 0.0) & (there > 0.0), -0.5 * (here + there), 0.0)
            coef[t, pl.ds(k, CX + 16, stride=8), :] = face
        coef[t, pl.ds(6, CX + 16, stride=8), :] = jnp.where(here > 0.0, 0.5 * total, 0.0)
        return carry

    lax.fori_loop(0, EXT_T, couplings, 0)

    for copy in copies + thirds:
        copy.wait_recv()

    def stencil(read, x, tiles, left, right, shift, emit):
        base = pl.multiple_of((x + 8 - REACH) * 8, 8)
        before = left
        value = read(x, tiles[0])
        turned = swap_halves(value)
        if before is None:
            before = turned
        for t in tiles:
            c = [
                jnp.broadcast_to(coef[t, pl.ds(base + k, 1), :], (SRC, LANES)) for k in range(7)
            ]
            if t == tiles[-1]:
                following, after = None, turned if right is None else right
            else:
                following = read(x, t + 1)
                after = swap_halves(following)
            diagonal = c[6] if shift == 0.0 else c[6] - shift
            total = diagonal * value
            total = total + c[0] * read(x - 1, t)
            total = total + c[1] * read(x + 1, t)
            total = total + c[2] * turned
            total = total + c[3] * jnp.where(low, before, after)
            total = total + c[4] * pltpu.roll(value, 1, 1)
            total = total + c[5] * pltpu.roll(value, LANES - 1, 1)
            emit(t, total)
            value, before, turned = following, turned, after

    spot = jnp.zeros((SRC, LANES), jnp.int32)
    source = lax.broadcasted_iota(jnp.int32, (SRC, LANES), 0)
    for k in range(SRC):
        spot = jnp.where(source == k, electrodes[k], spot)
    spot = spot - lane

    def first_row(x, carry):
        cell_x = gx * CX + x - REACH
        inside = (cell_x >= 0) & (cell_x < GX * CX)
        origin = (cell_x * (GY * TILES) + gy * TILES - 1) * LANES
        p = x - REACH
        centre = (p >= 0) & (p < CX)
        held = jnp.where(centre, lax.rem(p + CX // 2, CX // 2), 0)
        far = p >= CX // 2
        left = third_in[0, held]
        right = third_in[1, held]
        left = jnp.where(far, swap_halves(left), left)
        right = jnp.where(far, swap_halves(right), right)

        def emit(t, total):
            ok = inside
            if t == 0:
                ok = ok & (gy > 0)
            if t == EXT_T - 1:
                ok = ok & (gy < GY - 1)
            cell = jnp.where(ok, origin + t * LANES, -(2**30))
            field[x, pl.ds(0, SRC), tile(t)] = jnp.where(spot == cell, 20.0, 0.0) - total

        stencil(
            lambda i, t: start[i, :, tile(t)], x, range(EXT_T), left, right, 0.0, emit
        )
        return carry

    lax.fori_loop(1, EXT_X - 1, first_row, 0)

    def second_row(x, carry):
        def emit(t, total):
            field[x, pl.ds(SRC, SRC), tile(t)] = total

        stencil(
            lambda i, t: field[i, pl.ds(0, SRC), tile(t)], x, range(EXT_T), None, None, 0.8, emit
        )
        return carry

    lax.fori_loop(2, EXT_X - 2, second_row, 0)

    def third_row(x, carry):
        def read(i, t):
            return field[i, pl.ds(SRC, SRC), tile(t)]

        def emit(t, total):
            field[x, pl.ds(2 * SRC, SRC), tile(t)] = total

        left = swap_halves(read(x, 0))
        right = swap_halves(read(x, EXT_T - 1))
        stencil(read, x, range(1, TILES + 1), left, right, 1.6, emit)
        return carry

    lax.fori_loop(REACH, REACH + CX, third_row, 0)

    def products(x, total):
        values = field[x + REACH, :, pl.ds(LANES, MERGED)]
        coarse = values.astype(jnp.bfloat16)
        fine = (values - coarse.astype(f32)).astype(jnp.bfloat16)
        both = jnp.concatenate([coarse, fine], axis=0)
        split[x] = both
        return total + lax.dot_general(
            both, both, (((1,), (1,)), ((), ())), preferred_element_type=f32
        )

    total = lax.fori_loop(0, CX, products, jnp.zeros((2 * COLS, 2 * COLS), f32))
    store = pltpu.make_async_copy(split, cols, local_sem.at[2])
    store.start()
    total = total[:COLS] + total[COLS:]
    total = total[:, :COLS] + total[:, COLS:]
    empty = jnp.zeros((COLS // 2, HALF - COLS), f32)
    total = jnp.concatenate([total[: COLS // 2], empty, total[COLS // 2 :], empty], axis=1)

    for kind, (size, part) in enumerate(zip(GROUPS, (part0, part1, part2))):
        me = place(kind, gx, gy)
        part[me] = total
        sums = []
        for step in range(1, size):
            copy = pltpu.make_async_remote_copy(
                src_ref=part.at[me],
                dst_ref=part.at[me],
                send_sem=sum_send.at[kind, step],
                recv_sem=sum_recv.at[kind, size - step],
                device_id=partner(kind, gx, gy, step),
                device_id_type=MESH,
            )
            copy.start()
            sums.append(copy)
        for copy in sums:
            copy.wait()
        total = part[0]
        for i in range(1, size):
            total = total + part[i]
    gram[...] = total

    for copy in cond_copies + copies + thirds:
        copy.wait_send()
    store.wait()


def basis_kernel(cols, gram, basis, triangle, held, result, load_sem, store_sem):
    f32 = jnp.float32
    chunks = 8
    width = MERGED // chunks
    loads = [
        pltpu.make_async_copy(
            cols.at[:, :, pl.ds(i * width, width)],
            held.at[:, :, pl.ds(i * width, width)],
            load_sem.at[i],
        )
        for i in range(chunks)
    ]
    for load in loads:
        load.start()

    packed = gram[...]
    full = jnp.concatenate([packed, pltpu.roll(packed, HALF, 1)], axis=0)
    row = lax.broadcasted_iota(jnp.int32, (COLS, LANES), 0)
    lane = lax.broadcasted_iota(jnp.int32, (COLS, LANES), 1)
    matrix = jnp.where(lane < COLS, full, jnp.where(lane == row + HALF, 1.0, 0.0))
    pivots = jnp.ones((COLS, LANES), f32)
    for k in range(COLS):
        pivot_row = matrix[k : k + 1, :]
        pivot = pivot_row[:, k : k + 1]
        column = matrix[:, k : k + 1]
        pivots = jnp.where(row == k, pivot, pivots)
        if k < COLS - 1:
            factor = jnp.where(row > k, column * (1.0 / pivot), 0.0)
            matrix = matrix - factor * pivot_row
    matrix = matrix * lax.rsqrt(pivots)
    size = math.sqrt(GX * CX * GY * MERGED)
    upper = jnp.where((lane >= row) & (lane < COLS), matrix * (1.0 / size), 0.0)
    triangle[...] = upper[:, :COLS]
    inverse = pltpu.roll(matrix, HALF, 1)[:, :COLS] * size
    coarse = inverse.astype(jnp.bfloat16)
    fine = (inverse - coarse.astype(f32)).astype(jnp.bfloat16)
    weights = jnp.concatenate([coarse, coarse, fine], axis=1)

    stores = []
    for i in range(chunks):
        loads[i].wait()

        def one(x, carry):
            both = held[x, :, pl.ds(i * width, width)]
            stack = jnp.concatenate([both, both[:COLS]], axis=0)
            solved = jnp.dot(weights, stack, preferred_element_type=f32)
            for t in range(width // LANES):
                result[i * (width // LANES) + t, pl.ds(x, COLS, stride=CX), :] = solved[
                    :, t * LANES : (t + 1) * LANES
                ]
            return carry

        lax.fori_loop(0, CX, one, 0, unroll=True)
        for t in range(i * (width // LANES), (i + 1) * (width // LANES)):
            store = pltpu.make_async_copy(
                result.at[t], basis.at[:, tile(t)], store_sem.at[t]
            )
            store.start()
            stores.append(store)
    for store in stores:
        store.wait()


def per_device(initial_guess, conductivity, electrodes):
    f32 = jnp.float32
    any_space = pl.BlockSpec(memory_space=pltpu.HBM)
    vmem = pl.BlockSpec(memory_space=pltpu.VMEM)
    smem = pl.BlockSpec(memory_space=pltpu.SMEM)
    dma = pltpu.SemaphoreType.DMA
    cols, gram = pl.pallas_call(
        krylov_kernel,
        out_shape=(
            jax.ShapeDtypeStruct((CX, 2 * COLS, MERGED), jnp.bfloat16),
            jax.ShapeDtypeStruct((COLS // 2, LANES), f32),
        ),
        in_specs=[any_space, any_space, smem],
        out_specs=(any_space, vmem),
        scratch_shapes=[
            pltpu.VMEM((TILES, SRC * CX, LANES), f32),
            pltpu.VMEM((EXT_X, SRC, EXT), f32),
            pltpu.VMEM((EXT_X, COLS, EXT), f32),
            pltpu.VMEM((CX + 16, EXT + 2 * LANES), f32),
            pltpu.VMEM((EXT_T, (CX + 16) * 8, LANES), f32),
            pltpu.VMEM((2, CX // 2, SRC, LANES), f32),
            pltpu.VMEM((2, CX // 2, SRC, LANES), f32),
            pltpu.VMEM((CX, 2 * COLS, MERGED), jnp.bfloat16),
            pltpu.VMEM((GROUPS[0], COLS // 2, LANES), f32),
            pltpu.VMEM((GROUPS[1], COLS // 2, LANES), f32),
            pltpu.VMEM((GROUPS[2], COLS // 2, LANES), f32),
            dma((TILES,)),
            dma((3,)),
            dma((8,)),
            dma((8,)),
            dma((8,)),
            dma((8,)),
            dma((2,)),
            dma((2,)),
            dma((3, 8)),
            dma((3, 8)),
        ],
        compiler_params=pltpu.CompilerParams(
            collective_id=0, has_side_effects=True, vmem_limit_bytes=60 * 2**20
        ),
        name="krylov",
    )(initial_guess.reshape(SRC * CX, MERGED), conductivity, electrodes)
    basis, triangle = pl.pallas_call(
        basis_kernel,
        out_shape=(
            jax.ShapeDtypeStruct((COLS * CX, MERGED), f32),
            jax.ShapeDtypeStruct((COLS, COLS), f32),
        ),
        in_specs=[any_space, vmem],
        out_specs=(any_space, vmem),
        scratch_shapes=[
            pltpu.VMEM((CX, 2 * COLS, MERGED), jnp.bfloat16),
            pltpu.VMEM((TILES, COLS * CX, LANES), f32),
            dma((8,)),
            dma((TILES,)),
        ],
        compiler_params=pltpu.CompilerParams(vmem_limit_bytes=60 * 2**20),
        name="basis",
    )(cols, gram)
    return basis.reshape(COLS, CX, MERGED), triangle


def solution(mesh):
    return jax.shard_map(
        per_device,
        mesh=mesh,
        in_specs=(P(None, "gx", "gy"), P("gx", "gy"), P()),
        out_specs=(P(None, "gx", "gy"), P()),
        check_vma=False,
    )
```

```python
import functools
import math

import jax
import jax.numpy as jnp
from jax import lax
from jax.experimental import pallas as pl
from jax.experimental.pallas import tpu as pltpu
from jax.sharding import PartitionSpec as P

MESH = pl.DeviceIdType.MESH
NZ = 64
LANES = 128
HALF = 64
SRC = 16
COLS = 48
CX = 16
TILES = 16
REACH = 3
EXT_X = CX + 2 * REACH
EXT_T = TILES + 2
EXT = EXT_T * LANES
MERGED = TILES * LANES
GX, GY = 32, 8
MOVES = ((1, 0), (-1, 0), (0, 1), (0, -1), (1, 1), (1, -1), (-1, 1), (-1, -1))


def tile(t):
    if isinstance(t, int):
        return pl.ds(t * LANES, LANES)
    return pl.ds(pl.multiple_of(t * LANES, LANES), LANES)


def swap_halves(v):
    return pltpu.roll(v, HALF, 1)


def partner(kind, gx, gy, step):
    if kind == 0:
        base = (gx // 8) * 8
        return (base + lax.rem(gx - base + step, 8), gy)
    if kind == 1:
        return (lax.rem(gx + 8 * step, GX), gy)
    return (gx, lax.rem(gy + step, GY))


def place(kind, gx, gy):
    return (lax.rem(gx, 8), gx // 8, gy)[kind]


GROUPS = (8, 4, 8)


def krylov_kernel(
    guess,
    cond,
    electrodes,
    cols,
    gram,
    natural,
    start,
    field,
    field_s,
    field_t,
    cond_ext,
    coef,
    third_out,
    third_in,
    split,
    part0,
    part1,
    part2,
    guess_sem,
    local_sem,
    cond_send,
    cond_recv,
    send,
    recv,
    third_send_sem,
    third_recv_sem,
    sum_send,
    sum_recv,
):
    gx, gy = lax.axis_index("gx"), lax.axis_index("gy")
    f32 = jnp.float32

    def beside(move):
        dx, dy = move
        return (lax.rem(gx + dx + GX, GX), lax.rem(gy + dy + GY, GY))

    loads = [
        pltpu.make_async_copy(
            guess.at[:, h, :, tile(t)],
            natural.at[h, t].reshape(SRC, 8, LANES),
            guess_sem.at[h, t],
        )
        for h in range(2)
        for t in range(TILES)
    ]
    for load in loads:
        load.start()
    load_cond = pltpu.make_async_copy(
        cond, cond_ext.at[pl.ds(8, CX), pl.ds(2 * LANES, MERGED)], local_sem.at[1]
    )
    load_cond.start()

    barrier = pltpu.get_barrier_semaphore()
    for move in MOVES:
        pl.semaphore_signal(barrier, inc=1, device_id=beside(move), device_id_type=MESH)
    for kind, size in enumerate(GROUPS):
        for step in range(1, size):
            pl.semaphore_signal(
                barrier, inc=1, device_id=partner(kind, gx, gy, step), device_id_type=MESH
            )

    for x in (0, EXT_X - 1):
        for t in (0, EXT_T - 1):
            start[x, :, tile(t)] = jnp.zeros((SRC, LANES), f32)
    for x in (0, 8 + CX):
        for t in (0, EXT_T + 1):
            cond_ext[pl.ds(x, 8), tile(t)] = jnp.zeros((8, LANES), f32)

    for load in loads:
        load.wait()

    def lay_out(x, carry):
        half, rest = x // 8, lax.rem(x, 8)
        for t in range(TILES):
            start[x + REACH, :, tile(t + 1)] = natural[half, t, pl.ds(rest, SRC, stride=8), :]
        return carry

    lax.fori_loop(0, CX, lay_out, 0)

    lane = lax.broadcasted_iota(jnp.int32, (SRC, LANES), 1)
    low = lane < HALF

    def pack_third(x, carry):
        near, far = REACH + x, REACH + CX // 2 + x
        third_out[0, x] = jnp.where(
            low, swap_halves(start[near, :, tile(TILES - 1)]), start[far, :, tile(TILES - 1)]
        )
        third_out[1, x] = jnp.where(
            low, start[far, :, tile(2)], swap_halves(start[near, :, tile(2)])
        )
        return carry

    lax.fori_loop(0, CX // 2, pack_third, 0)

    pl.semaphore_wait(barrier, len(MOVES) + sum(GROUPS) - len(GROUPS))

    cond_copies = []
    for i, (dx, dy) in enumerate(MOVES):
        if dx == 0:
            rows_from, rows_to, rows = pl.ds(0, CX), pl.ds(8, CX), CX
        elif dx > 0:
            rows_from, rows_to = pl.ds(CX - 8, 8), pl.ds(0, 8)
        else:
            rows_from, rows_to = pl.ds(0, 8), pl.ds(8 + CX, 8)
        if dy == 0:
            lanes_from, lanes_to = pl.ds(0, MERGED), pl.ds(2 * LANES, MERGED)
        elif dx == 0:
            lanes_from = pl.ds(MERGED - 2 * LANES if dy > 0 else 0, 2 * LANES)
            lanes_to = pl.ds(0 if dy > 0 else (TILES + 2) * LANES, 2 * LANES)
        else:
            lanes_from = tile(TILES - 1 if dy > 0 else 0)
            lanes_to = tile(1 if dy > 0 else TILES + 2)
        cond_copies.append(
            pltpu.make_async_remote_copy(
                src_ref=cond.at[rows_from, lanes_from],
                dst_ref=cond_ext.at[rows_to, lanes_to],
                send_sem=cond_send.at[i],
                recv_sem=cond_recv.at[i],
                device_id=beside((dx, dy)),
                device_id_type=MESH,
            )
        )
    copies = []
    for i, (dx, dy) in enumerate(MOVES):
        depth = REACH if dy == 0 else 2
        if dx == 0:
            x_from, x_to = pl.ds(REACH, CX), pl.ds(REACH, CX)
        elif dx > 0:
            x_from, x_to = pl.ds(REACH + CX - depth, depth), pl.ds(REACH - depth, depth)
        else:
            x_from, x_to = pl.ds(REACH, depth), pl.ds(REACH + CX, depth)
        if dy == 0:
            lanes_from = lanes_to = pl.ds(LANES, MERGED)
        else:
            lanes_from = tile(TILES if dy > 0 else 1)
            lanes_to = tile(0 if dy > 0 else TILES + 1)
        copies.append(
            pltpu.make_async_remote_copy(
                src_ref=start.at[x_from, :, lanes_from],
                dst_ref=start.at[x_to, :, lanes_to],
                send_sem=send.at[i],
                recv_sem=recv.at[i],
                device_id=beside((dx, dy)),
                device_id_type=MESH,
            )
        )
    thirds = [
        pltpu.make_async_remote_copy(
            src_ref=third_out.at[i],
            dst_ref=third_in.at[i],
            send_sem=third_send_sem.at[i],
            recv_sem=third_recv_sem.at[i],
            device_id=beside(move),
            device_id_type=MESH,
        )
        for i, move in enumerate(((0, 1), (0, -1)))
    ]
    for copy in cond_copies + copies + thirds:
        copy.start()

    load_cond.wait()
    for copy in cond_copies:
        copy.wait_recv()
    row = lax.broadcasted_iota(jnp.int32, (CX + 16, LANES), 0)
    lane_c = lax.broadcasted_iota(jnp.int32, (CX + 16, LANES), 1)
    first_x, last_x = gx == 0, gx == GX - 1
    row_from = jnp.where(first_x, 8, 0)
    row_to = jnp.where(last_x, 8 + CX, 16 + CX)
    inside_x = (row >= row_from) & (row < row_to)
    tile_from = jnp.where(gy == 0, 2, 0)
    tile_to = jnp.where(gy == GY - 1, TILES + 2, TILES + 4)
    z = lax.rem(lane_c, HALF)
    low_c = lane_c < HALF

    def couplings(t, carry):
        def load(place):
            row_end = jnp.where((place >= tile_from) & (place < tile_to), row_to, 0)
            return jnp.where(inside_x & (row < row_end), cond_ext[:, tile(place)], 0.0)

        here = load(t + 1)
        below, above = load(t), load(t + 2)
        swapped = swap_halves(here)
        outer = jnp.where(low_c, swap_halves(below), swap_halves(above))
        z_down = jnp.where(z == 0, 0.0, pltpu.roll(here, 1, 1))
        z_up = jnp.where(z == HALF - 1, 0.0, pltpu.roll(here, LANES - 1, 1))
        x_down = pltpu.roll(here, 1, 0)
        x_up = pltpu.roll(here, CX + 15, 0)
        total = 6.0 * here
        for k, there in enumerate((x_down, x_up, swapped, outer, z_down, z_up)):
            total = total + there
            face = jnp.where((here > 0.0) & (there > 0.0), -0.5 * (here + there), 0.0)
            coef[t, pl.ds(k, CX + 16, stride=8), :] = face
        coef[t, pl.ds(6, CX + 16, stride=8), :] = jnp.where(here > 0.0, 0.5 * total, 0.0)
        return carry

    lax.fori_loop(0, EXT_T, couplings, 0)

    for copy in copies + thirds:
        copy.wait_recv()

    def stencil(read, x, tiles, left, right, shift, emit):
        base = pl.multiple_of((x + 8 - REACH) * 8, 8)
        before = left
        value = read(x, tiles[0])
        turned = swap_halves(value)
        if before is None:
            before = turned
        for t in tiles:
            c = [
                jnp.broadcast_to(coef[t, pl.ds(base + k, 1), :], (SRC, LANES)) for k in range(7)
            ]
            if t == tiles[-1]:
                following, after = None, turned if right is None else right
            else:
                following = read(x, t + 1)
                after = swap_halves(following)
            diagonal = c[6] if shift == 0.0 else c[6] - shift
            near = diagonal * value + c[2] * turned
            across = c[0] * read(x - 1, t) + c[1] * read(x + 1, t)
            along = c[4] * pltpu.roll(value, 1, 1) + c[5] * pltpu.roll(value, LANES - 1, 1)
            total = (near + across) + (along + c[3] * jnp.where(low, before, after))
            emit(t, total)
            value, before, turned = following, turned, after

    spot = jnp.zeros((SRC, LANES), jnp.int32)
    source = lax.broadcasted_iota(jnp.int32, (SRC, LANES), 0)
    for k in range(SRC):
        spot = jnp.where(source == k, electrodes[k], spot)
    spot = spot - lane

    def first_row(x, carry):
        cell_x = gx * CX + x - REACH
        inside = (cell_x >= 0) & (cell_x < GX * CX)
        origin = (cell_x * (GY * TILES) + gy * TILES - 1) * LANES
        p = x - REACH
        centre = (p >= 0) & (p < CX)
        held = jnp.where(centre, lax.rem(p + CX // 2, CX // 2), 0)
        far = p >= CX // 2
        left = third_in[0, held]
        right = third_in[1, held]
        left = jnp.where(far, swap_halves(left), left)
        right = jnp.where(far, swap_halves(right), right)

        def emit(t, total):
            ok = inside
            if t == 0:
                ok = ok & (gy > 0)
            if t == EXT_T - 1:
                ok = ok & (gy < GY - 1)
            cell = jnp.where(ok, origin + t * LANES, -(2**30))
            field[x, :, tile(t)] = jnp.where(spot == cell, 20.0, 0.0) - total

        stencil(
            lambda i, t: start[i, :, tile(t)], x, range(EXT_T), left, right, 0.0, emit
        )
        return carry


    def second_row(x, carry):
        def emit(t, total):
            field_s[x, :, tile(t)] = total

        stencil(
            lambda i, t: field[i, :, tile(t)], x, range(EXT_T), None, None, 0.8, emit
        )
        return carry


    def third_row(x, carry):
        def read(i, t):
            return field_s[i, :, tile(t)]

        def emit(t, total):
            field_t[x - REACH, :, tile(t)] = total

        left = swap_halves(read(x, 0))
        right = swap_halves(read(x, EXT_T - 1))
        stencil(read, x, range(1, TILES + 1), left, right, 1.6, emit)
        return carry


    def products(x, total):
        inner = pl.ds(LANES, MERGED)
        values = jnp.concatenate(
            [field[x + REACH, :, inner], field_s[x + REACH, :, inner], field_t[x, :, inner]], axis=0
        )
        coarse = values.astype(jnp.bfloat16)
        fine = (values - coarse.astype(f32)).astype(jnp.bfloat16)
        both = jnp.concatenate([coarse, fine], axis=0)
        split[x] = both
        return total + lax.dot_general(
            both, both, (((1,), (1,)), ((), ())), preferred_element_type=f32
        )

    def sweep(begin, end, stages, total):
        def step(x, total):
            if "products" in stages:
                total = products(x - 5 - REACH, total)
            if "third" in stages:
                third_row(x - 4, 0)
            if "second" in stages:
                second_row(x - 2, 0)
            if "first" in stages:
                first_row(x, 0)
            return total

        return lax.fori_loop(begin, end, step, total)

    total = jnp.zeros((2 * COLS, 2 * COLS), f32)
    last = EXT_X - 1
    sweep(1, 4, ("first",), 0)
    sweep(4, 7, ("first", "second"), 0)
    sweep(7, 8, ("first", "second", "third"), 0)
    total = sweep(8, last, ("first", "second", "third", "products"), total)
    total = sweep(last, last + 1, ("second", "third", "products"), total)
    total = sweep(last + 1, last + 2, ("third", "products"), total)
    total = sweep(last + 2, last + 3, ("products",), total)
    store = pltpu.make_async_copy(split, cols, local_sem.at[2])
    store.start()
    total = total[:COLS] + total[COLS:]
    total = total[:, :COLS] + total[:, COLS:]
    empty = jnp.zeros((COLS // 2, HALF - COLS), f32)
    total = jnp.concatenate([total[: COLS // 2], empty, total[COLS // 2 :], empty], axis=1)

    for kind, (size, part) in enumerate(zip(GROUPS, (part0, part1, part2))):
        me = place(kind, gx, gy)
        part[me] = total
        sums = []
        for step in range(1, size):
            copy = pltpu.make_async_remote_copy(
                src_ref=part.at[me],
                dst_ref=part.at[me],
                send_sem=sum_send.at[kind, step],
                recv_sem=sum_recv.at[kind, size - step],
                device_id=partner(kind, gx, gy, step),
                device_id_type=MESH,
            )
            copy.start()
            sums.append(copy)
        for copy in sums:
            copy.wait()
        total = part[0]
        for i in range(1, size):
            total = total + part[i]
    gram[...] = total

    for copy in cond_copies + copies + thirds:
        copy.wait_send()
    store.wait()


def basis_kernel(cols, gram, basis, triangle, held, result, load_sem, store_sem):
    f32 = jnp.float32
    chunks = 8
    width = MERGED // chunks

    def part(i):
        lanes = pl.ds(pl.multiple_of(i * width, width), width)
        return pltpu.make_async_copy(cols.at[:, :, lanes], held.at[:, :, lanes], load_sem.at[i])

    def begin(i, carry):
        part(i).start()
        return carry

    lax.fori_loop(0, chunks, begin, 0)

    packed = gram[...]
    full = jnp.concatenate([packed, pltpu.roll(packed, HALF, 1)], axis=0)
    row = lax.broadcasted_iota(jnp.int32, (8, LANES), 0)
    lane = lax.broadcasted_iota(jnp.int32, (8, LANES), 1)
    count = COLS // 8
    matrix = []
    for i in range(count):
        unit = jnp.where(lane == row + (HALF + 8 * i), 1.0, 0.0)
        matrix.append(jnp.where(lane < COLS, full[8 * i : 8 * i + 8], unit))
    pivots = [jnp.ones((8, LANES), f32) for _ in range(count)]

    def across(v, k):
        return jnp.broadcast_to(v[:, k : k + 1], (8, LANES))

    def down(v, r):
        return jnp.broadcast_to(v[r : r + 1, :], (8, LANES))

    for k in range(0, COLS, 2):
        block, r = k // 8, k % 8
        near = {i: across(matrix[i], k) for i in range(block, count)}
        far = {i: across(matrix[i], k + 1) for i in range(block, count)}
        row_near = down(matrix[block], r)
        row_far = down(matrix[block], r + 1)
        p, q, o = down(near[block], r), down(far[block], r + 1), down(far[block], r)
        inverse_near = 1.0 / p
        inverse_far = p / (p * q - o * o)
        ratio = o * inverse_near
        row_far = row_far - ratio * row_near
        for i in range(block, count):
            first = near[i] * inverse_near
            second = (far[i] - first * o) * inverse_far
            if i == block:
                second = jnp.where(row > r + 1, second, 0.0)
                pivots[i] = jnp.where(row == r, p, pivots[i])
                pivots[i] = jnp.where(row == r + 1, q - ratio * o, pivots[i])
                first = jnp.where(row > r, first, 0.0)
            matrix[i] = matrix[i] - (first * row_near + second * row_far)
    size = math.sqrt(GX * CX * GY * MERGED)
    matrix = jnp.concatenate([m * lax.rsqrt(p) for m, p in zip(matrix, pivots)], axis=0)
    row = lax.broadcasted_iota(jnp.int32, (COLS, LANES), 0)
    lane = lax.broadcasted_iota(jnp.int32, (COLS, LANES), 1)
    upper = jnp.where((lane >= row) & (lane < COLS), matrix * (1.0 / size), 0.0)
    triangle[...] = upper[:, :COLS]
    inverse = pltpu.roll(matrix, HALF, 1)[:, :COLS] * size
    coarse = inverse.astype(jnp.bfloat16)
    fine = (inverse - coarse.astype(f32)).astype(jnp.bfloat16)
    weights = jnp.concatenate([coarse, coarse, fine], axis=1)

    per_chunk = width // LANES

    def send(h, t):
        return pltpu.make_async_copy(
            result.at[h, t].reshape(COLS, 8, LANES), basis.at[:, h, :, tile(t)], store_sem.at[h, t]
        )

    def solve(i, carry):
        part(i).wait()
        lanes = pl.ds(pl.multiple_of(i * width, width), width)
        for x in range(CX):
            both = held[x, :, lanes]
            stack = jnp.concatenate([both, both[:COLS]], axis=0)
            solved = jnp.dot(weights, stack, preferred_element_type=f32)
            for t in range(per_chunk):
                result[x // 8, i * per_chunk + t, pl.ds(x % 8, COLS, stride=8), :] = solved[
                    :, t * LANES : (t + 1) * LANES
                ]
        for h in range(2):
            for t in range(per_chunk):
                send(h, i * per_chunk + t).start()
        return carry

    lax.fori_loop(0, chunks, solve, 0)

    def finish(t, carry):
        for h in range(2):
            send(h, t).wait()
        return carry

    lax.fori_loop(0, TILES, finish, 0)


def per_device(initial_guess, conductivity, electrodes):
    f32 = jnp.float32
    any_space = pl.BlockSpec(memory_space=pltpu.HBM)
    vmem = pl.BlockSpec(memory_space=pltpu.VMEM)
    smem = pl.BlockSpec(memory_space=pltpu.SMEM)
    dma = pltpu.SemaphoreType.DMA
    cols, gram = pl.pallas_call(
        krylov_kernel,
        out_shape=(
            jax.ShapeDtypeStruct((CX, 2 * COLS, MERGED), jnp.bfloat16),
            jax.ShapeDtypeStruct((COLS // 2, LANES), f32),
        ),
        in_specs=[any_space, any_space, smem],
        out_specs=(any_space, vmem),
        scratch_shapes=[
            pltpu.VMEM((2, TILES, SRC * 8, LANES), f32),
            pltpu.VMEM((EXT_X, SRC, EXT), f32),
            pltpu.VMEM((EXT_X, SRC, EXT), f32),
            pltpu.VMEM((EXT_X, SRC, EXT), f32),
            pltpu.VMEM((CX, SRC, EXT), f32),
            pltpu.VMEM((CX + 16, EXT + 2 * LANES), f32),
            pltpu.VMEM((EXT_T, (CX + 16) * 8, LANES), f32),
            pltpu.VMEM((2, CX // 2, SRC, LANES), f32),
            pltpu.VMEM((2, CX // 2, SRC, LANES), f32),
            pltpu.VMEM((CX, 2 * COLS, MERGED), jnp.bfloat16),
            pltpu.VMEM((GROUPS[0], COLS // 2, LANES), f32),
            pltpu.VMEM((GROUPS[1], COLS // 2, LANES), f32),
            pltpu.VMEM((GROUPS[2], COLS // 2, LANES), f32),
            dma((2, TILES)),
            dma((3,)),
            dma((8,)),
            dma((8,)),
            dma((8,)),
            dma((8,)),
            dma((2,)),
            dma((2,)),
            dma((3, 8)),
            dma((3, 8)),
        ],
        compiler_params=pltpu.CompilerParams(
            collective_id=0, has_side_effects=True, vmem_limit_bytes=60 * 2**20
        ),
        name="krylov",
    )(initial_guess.reshape(SRC, 2, 8, MERGED), conductivity, electrodes)
    basis, triangle = pl.pallas_call(
        basis_kernel,
        out_shape=(
            jax.ShapeDtypeStruct((COLS, 2, 8, MERGED), f32),
            jax.ShapeDtypeStruct((COLS, COLS), f32),
        ),
        in_specs=[any_space, vmem],
        out_specs=(any_space, vmem),
        scratch_shapes=[
            pltpu.VMEM((CX, 2 * COLS, MERGED), jnp.bfloat16),
            pltpu.VMEM((2, TILES, COLS * 8, LANES), f32),
            dma((8,)),
            dma((2, TILES)),
        ],
        compiler_params=pltpu.CompilerParams(vmem_limit_bytes=60 * 2**20),
        name="basis",
    )(cols, gram)
    return basis.reshape(COLS, CX, MERGED), triangle


def solution(mesh):
    return jax.shard_map(
        per_device,
        mesh=mesh,
        in_specs=(P(None, "gx", "gy"), P("gx", "gy"), P()),
        out_specs=(P(None, "gx", "gy"), P()),
        check_vma=False,
    )
```

```python
import functools
import math

import jax
import jax.numpy as jnp
from jax import lax
from jax.experimental import pallas as pl
from jax.experimental.pallas import tpu as pltpu
from jax.sharding import PartitionSpec as P

MESH = pl.DeviceIdType.MESH
NZ = 64
LANES = 128
HALF = 64
SRC = 16
COLS = 48
CX = 16
TILES = 16
REACH = 3
EXT_X = CX + 2 * REACH
EXT_T = TILES + 2
EXT = EXT_T * LANES
MERGED = TILES * LANES
GX, GY = 32, 8
MOVES = ((1, 0), (-1, 0), (0, 1), (0, -1), (1, 1), (1, -1), (-1, 1), (-1, -1))


def tile(t):
    if isinstance(t, int):
        return pl.ds(t * LANES, LANES)
    return pl.ds(pl.multiple_of(t * LANES, LANES), LANES)


def swap_halves(v):
    return pltpu.roll(v, HALF, 1)


def partner(kind, gx, gy, step):
    if kind == 0:
        base = (gx // 8) * 8
        return (base + lax.rem(gx - base + step, 8), gy)
    if kind == 1:
        return (lax.rem(gx + 8 * step, GX), gy)
    return (gx, lax.rem(gy + step, GY))


def place(kind, gx, gy):
    return (lax.rem(gx, 8), gx // 8, gy)[kind]


GROUPS = (8, 4, 8)


def krylov_kernel(
    guess,
    cond,
    electrodes,
    cols,
    gram,
    natural,
    start,
    field,
    field_s,
    field_t,
    cond_ext,
    coef,
    cond_out,
    cond_in,
    third_out,
    third_in,
    split,
    part0,
    part1,
    part2,
    guess_sem,
    local_sem,
    cond_send,
    cond_recv,
    send,
    recv,
    third_send_sem,
    third_recv_sem,
    sum_send,
    sum_recv,
):
    gx, gy = lax.axis_index("gx"), lax.axis_index("gy")
    f32 = jnp.float32

    def beside(move):
        dx, dy = move
        return (lax.rem(gx + dx + GX, GX), lax.rem(gy + dy + GY, GY))

    barrier = pltpu.get_barrier_semaphore()
    for move in MOVES:
        pl.semaphore_signal(barrier, inc=1, device_id=beside(move), device_id_type=MESH)

    def load(half, t):
        return pltpu.make_async_copy(
            guess.at[:, half, :, tile(t)],
            natural.at[half, t].reshape(SRC, 8, LANES),
            guess_sem.at[half, t],
        )

    def each_load(act):
        def step(t, carry):
            for half in range(2):
                act(load(half, t))
            return carry

        lax.fori_loop(0, TILES, step, 0)

    load_cond = pltpu.make_async_copy(
        cond, cond_ext.at[pl.ds(8, CX), pl.ds(2 * LANES, MERGED)], local_sem.at[1]
    )
    load_cond.start()
    each_load(lambda copy: copy.start())
    for kind, size in enumerate(GROUPS):
        for step in range(1, size):
            pl.semaphore_signal(
                barrier, inc=1, device_id=partner(kind, gx, gy, step), device_id_type=MESH
            )

    for x in (0, EXT_X - 1):
        for t in (0, EXT_T - 1):
            start[x, :, tile(t)] = jnp.zeros((SRC, LANES), f32)
    for x in (0, 8 + CX):
        for t in (0, EXT_T + 1):
            cond_ext[pl.ds(x, 8), tile(t)] = jnp.zeros((8, LANES), f32)
        cond_ext[pl.ds(x, 8), pl.ds(2 * LANES, MERGED)] = jnp.zeros((8, MERGED), f32)
    load_cond.wait()
    for i, x in enumerate((8 + CX - 4, 8)):
        cond_out[i] = cond_ext[pl.ds(x, 4), pl.ds(2 * LANES, MERGED)]

    each_load(lambda copy: copy.wait())

    def lay_out(x, carry):
        half, rest = x // 8, lax.rem(x, 8)
        for t in range(TILES):
            start[x + REACH, :, tile(t + 1)] = natural[half, t, pl.ds(rest, SRC, stride=8), :]
        return carry

    def lay_out_faces(x, carry):
        lay_out(x, 0)
        return lay_out(x + CX - REACH, carry)

    lax.fori_loop(0, REACH, lay_out_faces, 0)
    pl.semaphore_wait(barrier, len(MOVES) + sum(GROUPS) - len(GROUPS))

    cond_copies = []
    for i, (dx, dy) in enumerate(MOVES):
        if dx == 0:
            rows_from, rows_to = pl.ds(0, CX), pl.ds(8, CX)
        elif dx > 0:
            rows_from, rows_to = pl.ds(CX - 8, 8), pl.ds(0, 8)
        else:
            rows_from, rows_to = pl.ds(0, 8), pl.ds(8 + CX, 8)
        if dy == 0:
            lanes_from = lanes_to = pl.ds(0, MERGED)
        elif dx == 0:
            lanes_from = pl.ds(MERGED - 2 * LANES if dy > 0 else 0, 2 * LANES)
            lanes_to = pl.ds(0 if dy > 0 else (TILES + 2) * LANES, 2 * LANES)
        else:
            lanes_from = tile(TILES - 1 if dy > 0 else 0)
            lanes_to = tile(1 if dy > 0 else TILES + 2)
        source, target = cond.at[rows_from, lanes_from], cond_ext.at[rows_to, lanes_to]
        if dy == 0:
            side = 0 if dx > 0 else 1
            source, target = cond_out.at[side], cond_in.at[side]
        cond_copies.append(
            pltpu.make_async_remote_copy(
                src_ref=source,
                dst_ref=target,
                send_sem=cond_send.at[i],
                recv_sem=cond_recv.at[i],
                device_id=beside((dx, dy)),
                device_id_type=MESH,
            )
        )
    copies = []
    for i, (dx, dy) in enumerate(MOVES):
        depth = REACH if dy == 0 else 2
        if dx == 0:
            x_from, x_to = pl.ds(REACH, CX), pl.ds(REACH, CX)
        elif dx > 0:
            x_from, x_to = pl.ds(REACH + CX - depth, depth), pl.ds(REACH - depth, depth)
        else:
            x_from, x_to = pl.ds(REACH, depth), pl.ds(REACH + CX, depth)
        if dy == 0:
            lanes_from = lanes_to = pl.ds(LANES, MERGED)
        else:
            lanes_from = tile(TILES if dy > 0 else 1)
            lanes_to = tile(0 if dy > 0 else TILES + 1)
        copies.append(
            pltpu.make_async_remote_copy(
                src_ref=start.at[x_from, :, lanes_from],
                dst_ref=start.at[x_to, :, lanes_to],
                send_sem=send.at[i],
                recv_sem=recv.at[i],
                device_id=beside((dx, dy)),
                device_id_type=MESH,
            )
        )
    thirds = [
        pltpu.make_async_remote_copy(
            src_ref=third_out.at[i],
            dst_ref=third_in.at[i],
            send_sem=third_send_sem.at[i],
            recv_sem=third_recv_sem.at[i],
            device_id=beside(move),
            device_id_type=MESH,
        )
        for i, move in enumerate(((0, 1), (0, -1)))
    ]
    along_x = [copy for copy, (dx, dy) in zip(copies, MOVES) if dx != 0]
    along_y = [copy for copy, (dx, dy) in zip(copies, MOVES) if dx == 0]
    for copy in cond_copies + along_x:
        copy.start()

    lax.fori_loop(REACH, CX - REACH, lay_out, 0)
    lane = lax.broadcasted_iota(jnp.int32, (SRC, LANES), 1)
    low = lane < HALF

    def pack_third(x, carry):
        near, far = REACH + x, REACH + CX // 2 + x
        third_out[0, x] = jnp.where(
            low, swap_halves(start[near, :, tile(TILES - 1)]), start[far, :, tile(TILES - 1)]
        )
        third_out[1, x] = jnp.where(
            low, start[far, :, tile(2)], swap_halves(start[near, :, tile(2)])
        )
        return carry

    lax.fori_loop(0, CX // 2, pack_third, 0)

    for copy in along_y + thirds:
        copy.start()

    for copy in cond_copies:
        copy.wait_recv()
    for i, x in enumerate((4, 8 + CX)):
        cond_ext[pl.ds(x, 4), pl.ds(2 * LANES, MERGED)] = cond_in[i]
    row = lax.broadcasted_iota(jnp.int32, (CX + 16, LANES), 0)
    lane_c = lax.broadcasted_iota(jnp.int32, (CX + 16, LANES), 1)
    first_x, last_x = gx == 0, gx == GX - 1
    row_from = jnp.where(first_x, 8, 0)
    row_to = jnp.where(last_x, 8 + CX, 16 + CX)
    inside_x = (row >= row_from) & (row < row_to)
    tile_from = jnp.where(gy == 0, 2, 0)
    tile_to = jnp.where(gy == GY - 1, TILES + 2, TILES + 4)
    z = lax.rem(lane_c, HALF)
    low_c = lane_c < HALF

    def couplings(t, carry):
        def load(place):
            row_end = jnp.where((place >= tile_from) & (place < tile_to), row_to, 0)
            return jnp.where(inside_x & (row < row_end), cond_ext[:, tile(place)], 0.0)

        here = load(t + 1)
        below, above = load(t), load(t + 2)
        swapped = swap_halves(here)
        outer = jnp.where(low_c, swap_halves(below), swap_halves(above))
        z_down = jnp.where(z == 0, 0.0, pltpu.roll(here, 1, 1))
        z_up = jnp.where(z == HALF - 1, 0.0, pltpu.roll(here, LANES - 1, 1))
        x_down = pltpu.roll(here, 1, 0)
        x_up = pltpu.roll(here, CX + 15, 0)
        total = 6.0 * here
        for k, there in enumerate((x_down, x_up, swapped, outer, z_down, z_up)):
            total = total + there
            face = jnp.where((here > 0.0) & (there > 0.0), -0.5 * (here + there), 0.0)
            coef[t, pl.ds(k, CX + 16, stride=8), :] = face
        coef[t, pl.ds(6, CX + 16, stride=8), :] = jnp.where(here > 0.0, 0.5 * total, 0.0)
        return carry

    lax.fori_loop(0, EXT_T, couplings, 0)

    def stencil(read, x, runs, left, right, shift, emit):
        base = pl.multiple_of((x + 8 - REACH) * 8, 8)
        for begin, end in runs:
            value = read(x, begin)
            turned = swap_halves(value)
            before = left if begin == 0 else swap_halves(read(x, begin - 1))
            if before is None:
                before = turned
            for t in range(begin, end):
                c = [
                    jnp.broadcast_to(coef[t, pl.ds(base + k, 1), :], (SRC, LANES))
                    for k in range(7)
                ]
                if t == EXT_T - 1:
                    following, after = None, turned if right is None else right
                else:
                    following = read(x, t + 1)
                    after = swap_halves(following)
                diagonal = c[6] if shift == 0.0 else c[6] - shift
                near = diagonal * value + c[2] * turned
                across = c[0] * read(x - 1, t) + c[1] * read(x + 1, t)
                along = c[4] * pltpu.roll(value, 1, 1) + c[5] * pltpu.roll(value, LANES - 1, 1)
                total = (near + across) + (along + c[3] * jnp.where(low, before, after))
                emit(t, total)
                value, before, turned = following, turned, after

    spot = jnp.zeros((SRC, LANES), jnp.int32)
    source = lax.broadcasted_iota(jnp.int32, (SRC, LANES), 0)
    for k in range(SRC):
        spot = jnp.where(source == k, electrodes[k], spot)
    spot = spot - lane

    def outer_thirds(x):
        p = x - REACH
        centre = (p >= 0) & (p < CX)
        held = jnp.where(centre, lax.rem(p + CX // 2, CX // 2), 0)
        far = p >= CX // 2
        left = third_in[0, held]
        right = third_in[1, held]
        left = jnp.where(far, swap_halves(left), left)
        right = jnp.where(far, swap_halves(right), right)
        return left, right

    def first_row(x, runs):
        cell_x = gx * CX + x - REACH
        inside = (cell_x >= 0) & (cell_x < GX * CX)
        origin = (cell_x * (GY * TILES) + gy * TILES - 1) * LANES
        left = right = None
        if runs[0][0] == 0:
            left, right = outer_thirds(x)

        def emit(t, total):
            ok = inside
            if t == 0:
                ok = ok & (gy > 0)
            if t == EXT_T - 1:
                ok = ok & (gy < GY - 1)
            cell = jnp.where(ok, origin + t * LANES, -(2**30))
            field[x, :, tile(t)] = jnp.where(spot == cell, 20.0, 0.0) - total

        stencil(lambda i, t: start[i, :, tile(t)], x, runs, left, right, 0.0, emit)


    def second_row(x, runs):
        def emit(t, total):
            field_s[x, :, tile(t)] = total

        stencil(lambda i, t: field[i, :, tile(t)], x, runs, None, None, 0.8, emit)

    def third_row(x, runs):
        def read(i, t):
            return field_s[i, :, tile(t)]

        def emit(t, total):
            field_t[x - REACH, :, tile(t)] = total

        stencil(read, x, runs, None, None, 1.6, emit)

    def products(x, runs, total):
        pieces = []
        for begin, end in runs:
            inner = pl.ds(begin * LANES, (end - begin) * LANES)
            values = jnp.concatenate(
                [field[x, :, inner], field_s[x, :, inner], field_t[x - REACH, :, inner]], axis=0
            )
            coarse = values.astype(jnp.bfloat16)
            fine = (values - coarse.astype(f32)).astype(jnp.bfloat16)
            both = jnp.concatenate([coarse, fine], axis=0)
            split[x - REACH, :, pl.ds((begin - 1) * LANES, (end - begin) * LANES)] = both
            pieces.append(both)
        both = pieces[0] if len(pieces) == 1 else jnp.concatenate(pieces, axis=1)
        return total + lax.dot_general(
            both, both, (((1,), (1,)), ((), ())), preferred_element_type=f32
        )

    def sweep(begin, end, total, first=None, second=None, third=None, inner=None):
        def step(x, total):
            if inner:
                total = products(x - 5, inner, total)
            if third:
                third_row(x - 4, third)
            if second:
                second_row(x - 2, second)
            if first:
                first_row(x, first)
            return total

        return lax.fori_loop(begin, end, step, total)

    total = jnp.zeros((2 * COLS, 2 * COLS), f32)
    f, s, t, p = ((2, 16),), ((3, 15),), ((4, 14),), ((4, 14),)
    sweep(4, 7, 0, f)
    sweep(7, 10, 0, f, s)
    sweep(10, 11, 0, f, s, t)
    total = sweep(11, 18, total, f, s, t, p)
    total = sweep(18, 19, total, None, s, t, p)
    total = sweep(19, 20, total, None, None, t, p)
    total = sweep(20, 21, total, None, None, None, p)

    for copy in copies + thirds:
        copy.wait_recv()

    f, s, t, p = ((0, 18),), ((0, 18),), ((1, 17),), ((1, 17),)
    f_rim, s_rim = ((0, 2), (16, 18)), ((0, 3), (15, 18))
    t_rim = p_rim = ((1, 4), (14, 17))
    sweep(1, 4, 0, f)
    sweep(4, 7, 0, f_rim, s)
    sweep(7, 8, 0, f_rim, s_rim, t)
    total = sweep(8, 11, total, f_rim, s_rim, t, p)
    total = sweep(11, 18, total, f_rim, s_rim, t_rim, p_rim)
    total = sweep(18, 21, total, f, s, t, p_rim)
    total = sweep(21, 22, total, None, s, t, p)
    total = sweep(22, 23, total, None, None, t, p)
    total = sweep(23, 24, total, None, None, None, p)
    store = pltpu.make_async_copy(split, cols, local_sem.at[2])
    store.start()
    total = total[:COLS] + total[COLS:]
    total = total[:, :COLS] + total[:, COLS:]
    empty = jnp.zeros((COLS // 2, HALF - COLS), f32)
    total = jnp.concatenate([total[: COLS // 2], empty, total[COLS // 2 :], empty], axis=1)

    for kind, (size, part) in enumerate(zip(GROUPS, (part0, part1, part2))):
        me = place(kind, gx, gy)
        part[me] = total
        sums = []
        for step in range(1, size):
            copy = pltpu.make_async_remote_copy(
                src_ref=part.at[me],
                dst_ref=part.at[me],
                send_sem=sum_send.at[kind, step],
                recv_sem=sum_recv.at[kind, size - step],
                device_id=partner(kind, gx, gy, step),
                device_id_type=MESH,
            )
            copy.start()
            sums.append(copy)
        for copy in sums:
            copy.wait()
        total = part[0]
        for i in range(1, size):
            total = total + part[i]
    gram[...] = total

    for copy in cond_copies + copies + thirds:
        copy.wait_send()
    store.wait()


def basis_kernel(cols, gram, basis, triangle, held, result, load_sem, store_sem):
    f32 = jnp.float32
    chunks = 8
    width = MERGED // chunks

    def part(i):
        lanes = pl.ds(pl.multiple_of(i * width, width), width)
        return pltpu.make_async_copy(cols.at[:, :, lanes], held.at[:, :, lanes], load_sem.at[i])

    def begin(i, carry):
        part(i).start()
        return carry

    lax.fori_loop(0, chunks, begin, 0)

    packed = gram[...]
    full = jnp.concatenate([packed, pltpu.roll(packed, HALF, 1)], axis=0)
    row = lax.broadcasted_iota(jnp.int32, (8, LANES), 0)
    lane = lax.broadcasted_iota(jnp.int32, (8, LANES), 1)
    count = COLS // 8
    matrix = []
    for i in range(count):
        unit = jnp.where(lane == row + (HALF + 8 * i), 1.0, 0.0)
        matrix.append(jnp.where(lane < COLS, full[8 * i : 8 * i + 8], unit))
    pivots = [jnp.ones((8, LANES), f32) for _ in range(count)]

    def across(v, k):
        return jnp.broadcast_to(v[:, k : k + 1], (8, LANES))

    def down(v, r):
        return jnp.broadcast_to(v[r : r + 1, :], (8, LANES))

    for k in range(0, COLS, 2):
        block, r = k // 8, k % 8
        near = {i: across(matrix[i], k) for i in range(block, count)}
        far = {i: across(matrix[i], k + 1) for i in range(block, count)}
        row_near = down(matrix[block], r)
        row_far = down(matrix[block], r + 1)
        p, q, o = down(near[block], r), down(far[block], r + 1), down(far[block], r)
        inverse_near = 1.0 / p
        inverse_far = p / (p * q - o * o)
        ratio = o * inverse_near
        row_far = row_far - ratio * row_near
        for i in range(block, count):
            first = near[i] * inverse_near
            second = (far[i] - first * o) * inverse_far
            if i == block:
                second = jnp.where(row > r + 1, second, 0.0)
                pivots[i] = jnp.where(row == r, p, pivots[i])
                pivots[i] = jnp.where(row == r + 1, q - ratio * o, pivots[i])
                first = jnp.where(row > r, first, 0.0)
            matrix[i] = matrix[i] - (first * row_near + second * row_far)
    size = math.sqrt(GX * CX * GY * MERGED)
    matrix = jnp.concatenate([m * lax.rsqrt(p) for m, p in zip(matrix, pivots)], axis=0)
    row = lax.broadcasted_iota(jnp.int32, (COLS, LANES), 0)
    lane = lax.broadcasted_iota(jnp.int32, (COLS, LANES), 1)
    upper = jnp.where((lane >= row) & (lane < COLS), matrix * (1.0 / size), 0.0)
    triangle[...] = upper[:, :COLS]
    inverse = pltpu.roll(matrix, HALF, 1)[:, :COLS] * size
    coarse = inverse.astype(jnp.bfloat16)
    fine = (inverse - coarse.astype(f32)).astype(jnp.bfloat16)
    weights = jnp.concatenate([coarse, coarse, fine], axis=1)

    per_chunk = width // LANES

    def send(h, t):
        return pltpu.make_async_copy(
            result.at[h, t].reshape(COLS, 8, LANES), basis.at[:, h, :, tile(t)], store_sem.at[h, t]
        )

    def solve(i, carry):
        part(i).wait()
        lanes = pl.ds(pl.multiple_of(i * width, width), width)
        for x in range(CX):
            both = held[x, :, lanes]
            stack = jnp.concatenate([both, both[:COLS]], axis=0)
            solved = jnp.dot(weights, stack, preferred_element_type=f32)
            for t in range(per_chunk):
                result[x // 8, i * per_chunk + t, pl.ds(x % 8, COLS, stride=8), :] = solved[
                    :, t * LANES : (t + 1) * LANES
                ]
        for h in range(2):
            for t in range(per_chunk):
                send(h, i * per_chunk + t).start()
        return carry

    lax.fori_loop(0, chunks, solve, 0)

    def finish(t, carry):
        for h in range(2):
            send(h, t).wait()
        return carry

    lax.fori_loop(0, TILES, finish, 0)


def per_device(initial_guess, conductivity, electrodes):
    f32 = jnp.float32
    any_space = pl.BlockSpec(memory_space=pltpu.HBM)
    vmem = pl.BlockSpec(memory_space=pltpu.VMEM)
    smem = pl.BlockSpec(memory_space=pltpu.SMEM)
    dma = pltpu.SemaphoreType.DMA
    cols, gram = pl.pallas_call(
        krylov_kernel,
        out_shape=(
            jax.ShapeDtypeStruct((CX, 2 * COLS, MERGED), jnp.bfloat16),
            jax.ShapeDtypeStruct((COLS // 2, LANES), f32),
        ),
        in_specs=[any_space, any_space, smem],
        out_specs=(any_space, vmem),
        scratch_shapes=[
            pltpu.VMEM((2, TILES, SRC * 8, LANES), f32),
            pltpu.VMEM((EXT_X, SRC, EXT), f32),
            pltpu.VMEM((EXT_X, SRC, EXT), f32),
            pltpu.VMEM((EXT_X, SRC, EXT), f32),
            pltpu.VMEM((CX, SRC, EXT), f32),
            pltpu.VMEM((CX + 16, EXT + 2 * LANES), f32),
            pltpu.VMEM((EXT_T, (CX + 16) * 8, LANES), f32),
            pltpu.VMEM((2, 4, MERGED), f32),
            pltpu.VMEM((2, 4, MERGED), f32),
            pltpu.VMEM((2, CX // 2, SRC, LANES), f32),
            pltpu.VMEM((2, CX // 2, SRC, LANES), f32),
            pltpu.VMEM((CX, 2 * COLS, MERGED), jnp.bfloat16),
            pltpu.VMEM((GROUPS[0], COLS // 2, LANES), f32),
            pltpu.VMEM((GROUPS[1], COLS // 2, LANES), f32),
            pltpu.VMEM((GROUPS[2], COLS // 2, LANES), f32),
            dma((2, TILES)),
            dma((3,)),
            dma((8,)),
            dma((8,)),
            dma((8,)),
            dma((8,)),
            dma((2,)),
            dma((2,)),
            dma((3, 8)),
            dma((3, 8)),
        ],
        compiler_params=pltpu.CompilerParams(
            collective_id=0, has_side_effects=True, vmem_limit_bytes=60 * 2**20
        ),
        name="krylov",
    )(initial_guess.reshape(SRC, 2, 8, MERGED), conductivity, electrodes)
    basis, triangle = pl.pallas_call(
        basis_kernel,
        out_shape=(
            jax.ShapeDtypeStruct((COLS, 2, 8, MERGED), f32),
            jax.ShapeDtypeStruct((COLS, COLS), f32),
        ),
        in_specs=[any_space, vmem],
        out_specs=(any_space, vmem),
        scratch_shapes=[
            pltpu.VMEM((CX, 2 * COLS, MERGED), jnp.bfloat16),
            pltpu.VMEM((2, TILES, COLS * 8, LANES), f32),
            dma((8,)),
            dma((2, TILES)),
        ],
        compiler_params=pltpu.CompilerParams(vmem_limit_bytes=60 * 2**20),
        name="basis",
    )(cols, gram)
    return basis.reshape(COLS, CX, MERGED), triangle


def solution(mesh):
    return jax.shard_map(
        per_device,
        mesh=mesh,
        in_specs=(P(None, "gx", "gy"), P("gx", "gy"), P()),
        out_specs=(P(None, "gx", "gy"), P()),
        check_vma=False,
    )
```

```python
import functools
import math

import jax
import jax.numpy as jnp
from jax import lax
from jax.experimental import pallas as pl
from jax.experimental.pallas import tpu as pltpu
from jax.sharding import PartitionSpec as P

MESH = pl.DeviceIdType.MESH
NZ = 64
SHARE = 2
LANES = 128
HALF = 64
SRC = 16
COLS = 48
CX = 16
TILES = 16
REACH = 3
EXT_X = CX + 2 * REACH
EXT_T = TILES + 2
EXT = EXT_T * LANES
MERGED = TILES * LANES
GX, GY = 32, 8
MOVES = ((1, 0), (-1, 0), (0, 1), (0, -1), (1, 1), (1, -1), (-1, 1), (-1, -1))


def tile(t):
    if isinstance(t, int):
        return pl.ds(t * LANES, LANES)
    return pl.ds(pl.multiple_of(t * LANES, LANES), LANES)


def swap_halves(v):
    return pltpu.roll(v, HALF, 1)


def partner(kind, gx, gy, step):
    if kind == 0:
        base = (gx // 8) * 8
        return (base + lax.rem(gx - base + step, 8), gy)
    if kind == 1:
        return (lax.rem(gx + 8 * step, GX), gy)
    return (gx, lax.rem(gy + step, GY))


def place(kind, gx, gy):
    return (lax.rem(gx, 8), gx // 8, gy)[kind]


GROUPS = (8, 4, 8)


def krylov_kernel(
    guess,
    cond,
    electrodes,
    cols,
    gram,
    natural,
    start,
    field,
    field_s,
    field_t,
    cond_ext,
    coef,
    shifts,
    cond_out,
    cond_in,
    third_out,
    third_in,
    split,
    part0,
    part1,
    part2,
    guess_sem,
    local_sem,
    cond_send,
    cond_recv,
    send,
    recv,
    third_send_sem,
    third_recv_sem,
    sum_send,
    sum_recv,
):
    gx, gy = lax.axis_index("gx"), lax.axis_index("gy")
    f32 = jnp.float32

    def beside(move):
        dx, dy = move
        return (lax.rem(gx + dx + GX, GX), lax.rem(gy + dy + GY, GY))

    barrier = pltpu.get_barrier_semaphore()
    for move in MOVES:
        pl.semaphore_signal(barrier, inc=1, device_id=beside(move), device_id_type=MESH)

    def load(half, t):
        return pltpu.make_async_copy(
            guess.at[:, half, :, tile(t)],
            natural.at[half, t].reshape(SRC, 8, LANES),
            guess_sem.at[half, t],
        )

    def each_load(act):
        def step(t, carry):
            for half in range(2):
                act(load(half, t))
            return carry

        lax.fori_loop(0, TILES, step, 0)

    load_cond = pltpu.make_async_copy(
        cond, cond_ext.at[pl.ds(8, CX), pl.ds(2 * LANES, MERGED)], local_sem.at[1]
    )
    load_cond.start()
    each_load(lambda copy: copy.start())
    for kind, size in enumerate(GROUPS):
        for step in range(1, size):
            pl.semaphore_signal(
                barrier, inc=1, device_id=partner(kind, gx, gy, step), device_id_type=MESH
            )

    for x in (0, EXT_X - 1):
        for t in (0, EXT_T - 1):
            start[x, :, tile(t)] = jnp.zeros((SRC, LANES), f32)
    for x in (0, 8 + CX):
        for t in (0, EXT_T + 1):
            cond_ext[pl.ds(x, 8), tile(t)] = jnp.zeros((8, LANES), f32)
        cond_ext[pl.ds(x, 8), pl.ds(2 * LANES, MERGED)] = jnp.zeros((8, MERGED), f32)
    load_cond.wait()
    for i, x in enumerate((8 + CX - 4, 8)):
        cond_out[i] = cond_ext[pl.ds(x, 4), pl.ds(2 * LANES, MERGED)]

    pl.semaphore_wait(barrier, len(MOVES) + sum(GROUPS) - len(GROUPS))

    cond_copies = []
    for i, (dx, dy) in enumerate(MOVES):
        if dx == 0:
            rows_from, rows_to = pl.ds(0, CX), pl.ds(8, CX)
        elif dx > 0:
            rows_from, rows_to = pl.ds(CX - 8, 8), pl.ds(0, 8)
        else:
            rows_from, rows_to = pl.ds(0, 8), pl.ds(8 + CX, 8)
        if dy == 0:
            lanes_from = lanes_to = pl.ds(0, MERGED)
        elif dx == 0:
            lanes_from = pl.ds(MERGED - 2 * LANES if dy > 0 else 0, 2 * LANES)
            lanes_to = pl.ds(0 if dy > 0 else (TILES + 2) * LANES, 2 * LANES)
        else:
            lanes_from = tile(TILES - 1 if dy > 0 else 0)
            lanes_to = tile(1 if dy > 0 else TILES + 2)
        source, target = cond.at[rows_from, lanes_from], cond_ext.at[rows_to, lanes_to]
        if dy == 0:
            side = 0 if dx > 0 else 1
            source, target = cond_out.at[side], cond_in.at[side]
        cond_copies.append(
            pltpu.make_async_remote_copy(
                src_ref=source,
                dst_ref=target,
                send_sem=cond_send.at[i],
                recv_sem=cond_recv.at[i],
                device_id=beside((dx, dy)),
                device_id_type=MESH,
            )
        )
    for copy in cond_copies:
        copy.start()

    each_load(lambda copy: copy.wait())

    def lay_out(x, carry):
        half, rest = x // 8, lax.rem(x, 8)
        for t in range(TILES):
            start[x + REACH, :, tile(t + 1)] = natural[half, t, pl.ds(rest, SRC, stride=8), :]
        return carry

    def lay_out_faces(x, carry):
        lay_out(x, 0)
        return lay_out(x + CX - REACH, carry)

    lax.fori_loop(0, REACH, lay_out_faces, 0)

    copies = []
    for i, (dx, dy) in enumerate(MOVES):
        depth = REACH if dy == 0 else 2
        if dx == 0:
            x_from, x_to = pl.ds(REACH, CX), pl.ds(REACH, CX)
        elif dx > 0:
            x_from, x_to = pl.ds(REACH + CX - depth, depth), pl.ds(REACH - depth, depth)
        else:
            x_from, x_to = pl.ds(REACH, depth), pl.ds(REACH + CX, depth)
        if dy == 0:
            lanes_from = lanes_to = pl.ds(LANES, MERGED)
        else:
            lanes_from = tile(TILES if dy > 0 else 1)
            lanes_to = tile(0 if dy > 0 else TILES + 1)
        copies.append(
            pltpu.make_async_remote_copy(
                src_ref=start.at[x_from, :, lanes_from],
                dst_ref=start.at[x_to, :, lanes_to],
                send_sem=send.at[i],
                recv_sem=recv.at[i],
                device_id=beside((dx, dy)),
                device_id_type=MESH,
            )
        )
    thirds = [
        pltpu.make_async_remote_copy(
            src_ref=third_out.at[i],
            dst_ref=third_in.at[i],
            send_sem=third_send_sem.at[i],
            recv_sem=third_recv_sem.at[i],
            device_id=beside(move),
            device_id_type=MESH,
        )
        for i, move in enumerate(((0, 1), (0, -1)))
    ]
    along_x = [copy for copy, (dx, dy) in zip(copies, MOVES) if dx != 0]
    along_y = [copy for copy, (dx, dy) in zip(copies, MOVES) if dx == 0]
    for copy in along_x:
        copy.start()

    lax.fori_loop(REACH, CX - REACH, lay_out, 0)
    lane = lax.broadcasted_iota(jnp.int32, (SRC, LANES), 1)
    low = lane < HALF

    def pack_third(x, carry):
        near, far = REACH + x, REACH + CX // 2 + x
        third_out[0, x] = jnp.where(
            low, swap_halves(start[near, :, tile(TILES - 1)]), start[far, :, tile(TILES - 1)]
        )
        third_out[1, x] = jnp.where(
            low, start[far, :, tile(2)], swap_halves(start[near, :, tile(2)])
        )
        return carry

    lax.fori_loop(0, CX // 2, pack_third, 0)

    for copy in along_y + thirds:
        copy.start()

    for copy in cond_copies:
        copy.wait_recv()
    for i, x in enumerate((4, 8 + CX)):
        cond_ext[pl.ds(x, 4), pl.ds(2 * LANES, MERGED)] = cond_in[i]
    row = lax.broadcasted_iota(jnp.int32, (CX + 16, LANES), 0)
    lane_c = lax.broadcasted_iota(jnp.int32, (CX + 16, LANES), 1)
    first_x, last_x = gx == 0, gx == GX - 1
    row_from = jnp.where(first_x, 8, 0)
    row_to = jnp.where(last_x, 8 + CX, 16 + CX)
    inside_x = (row >= row_from) & (row < row_to)
    tile_from = jnp.where(gy == 0, 2, 0)
    tile_to = jnp.where(gy == GY - 1, TILES + 2, TILES + 4)
    z = lax.rem(lane_c, HALF)
    low_c = lane_c < HALF

    def couplings(t, carry):
        def load(place):
            row_end = jnp.where((place >= tile_from) & (place < tile_to), row_to, 0)
            return jnp.where(inside_x & (row < row_end), cond_ext[:, tile(place)], 0.0)

        here = load(t + 1)
        below, above = load(t), load(t + 2)
        swapped = swap_halves(here)
        outer = jnp.where(low_c, swap_halves(below), swap_halves(above))
        z_down = jnp.where(z == 0, 0.0, pltpu.roll(here, 1, 1))
        z_up = jnp.where(z == HALF - 1, 0.0, pltpu.roll(here, LANES - 1, 1))
        x_down = pltpu.roll(here, 1, 0)
        x_up = pltpu.roll(here, CX + 15, 0)
        total = 6.0 * here
        for k, there in enumerate((x_down, x_up, swapped, outer, z_down, z_up)):
            total = total + there
            face = jnp.where((here > 0.0) & (there > 0.0), -0.5 * (here + there), 0.0)
            coef[t, pl.ds(k, CX + 16, stride=8), :] = face
        coef[t, pl.ds(6, CX + 16, stride=8), :] = jnp.where(here > 0.0, 0.5 * total, 0.0)
        return carry

    lax.fori_loop(0, EXT_T, couplings, 0)

    inward = lax.rem(lax.broadcasted_iota(jnp.int32, (2 * LANES, 2 * LANES), 0), LANES)
    outward = lax.broadcasted_iota(jnp.int32, (2 * LANES, 2 * LANES), 1)
    outward = jnp.where(outward < LANES, outward - 1, outward - (LANES - 1))
    shifts[...] = jnp.where(inward == outward, 1.0, 0.0).astype(jnp.bfloat16)

    def along_z(values):
        values = jnp.concatenate(values, axis=0)
        coarse = values.astype(jnp.bfloat16)
        fine = (values - coarse.astype(f32)).astype(jnp.bfloat16)
        both = jnp.concatenate([coarse, fine], axis=1)
        return jnp.dot(both, shifts[...], preferred_element_type=f32)

    def around(read, jobs):
        places = [
            (x, t)
            for x, runs in jobs
            for begin, end in runs
            for t in range(begin, end)
            if t % SHARE == 1
        ]
        both = along_z([read(x, t) for x, t in places])
        found = []
        for x, runs in jobs:
            row = {}
            for begin, end in runs:
                for t in range(begin, end):
                    if t % SHARE == 1:
                        row[t] = both[:SRC, :LANES], both[:SRC, LANES:]
                        both = both[SRC:]
            found.append(row)
        return found

    def stencil(read, x, runs, left, right, shift, emit, beside_z, closed=False):
        base = pl.multiple_of((x + 8 - REACH) * 8, 8)
        for begin, end in runs:
            value = read(x, begin)
            turned = swap_halves(value)
            if closed:
                before = turned
            elif begin > 0:
                before = swap_halves(read(x, begin - 1))
            else:
                before = turned if left is None else left
            for t in range(begin, end):
                c = [
                    jnp.broadcast_to(coef[t, pl.ds(base + k, 1), :], (SRC, LANES))
                    for k in range(7)
                ]
                if closed and t == end - 1:
                    following, after = None, turned
                elif t == EXT_T - 1:
                    following, after = None, turned if right is None else right
                else:
                    following = read(x, t + 1)
                    after = swap_halves(following)
                diagonal = c[6] if shift == 0.0 else c[6] - shift
                if t in beside_z:
                    z_down, z_up = beside_z[t]
                else:
                    z_down, z_up = pltpu.roll(value, 1, 1), pltpu.roll(value, LANES - 1, 1)
                near = diagonal * value + c[2] * turned
                across = c[0] * read(x - 1, t) + c[1] * read(x + 1, t)
                along = c[4] * z_down + c[5] * z_up
                total = (near + across) + (along + c[3] * jnp.where(low, before, after))
                emit(t, total)
                value, before, turned = following, turned, after

    spot = jnp.zeros((SRC, LANES), jnp.int32)
    source = lax.broadcasted_iota(jnp.int32, (SRC, LANES), 0)
    for k in range(SRC):
        spot = jnp.where(source == k, electrodes[k], spot)
    spot = spot - lane

    def outer_thirds(x):
        p = x - REACH
        centre = (p >= 0) & (p < CX)
        held = jnp.where(centre, lax.rem(p + CX // 2, CX // 2), 0)
        far = p >= CX // 2
        left = third_in[0, held]
        right = third_in[1, held]
        left = jnp.where(far, swap_halves(left), left)
        right = jnp.where(far, swap_halves(right), right)
        return left, right

    def read_start(x, t):
        return start[x, :, tile(t)]

    def first_rows(jobs):
        for (x, runs), beside_z in zip(jobs, around(read_start, jobs)):
            first_row(x, runs, beside_z)

    def first_row(x, runs, beside_z):
        cell_x = gx * CX + x - REACH
        inside = (cell_x >= 0) & (cell_x < GX * CX)
        origin = (cell_x * (GY * TILES) + gy * TILES - 1) * LANES
        left = right = None
        if runs[0][0] == 0:
            left, right = outer_thirds(x)

        def emit(t, total):
            ok = inside
            if t == 0:
                ok = ok & (gy > 0)
            if t == EXT_T - 1:
                ok = ok & (gy < GY - 1)
            cell = jnp.where(ok, origin + t * LANES, -(2**30))
            field[x, :, tile(t)] = jnp.where(spot == cell, 20.0, 0.0) - total

        closed = runs[0][0] == 1
        stencil(read_start, x, runs, left, right, 0.0, emit, beside_z, closed)


    def read_first(x, t):
        return field[x, :, tile(t)]

    def second_rows(jobs):
        for (x, runs), beside_z in zip(jobs, around(read_first, jobs)):
            second_row(x, runs, beside_z)

    def second_row(x, runs, beside_z):
        def emit(t, total):
            field_s[x, :, tile(t)] = total

        stencil(read_first, x, runs, None, None, 0.8, emit, beside_z)

    def read_second(x, t):
        return field_s[x, :, tile(t)]

    def third_rows(jobs):
        for (x, runs), beside_z in zip(jobs, around(read_second, jobs)):
            third_row(x, runs, beside_z)

    def third_row(x, runs, beside_z):
        def emit(t, total):
            field_t[x - REACH, :, tile(t)] = total

        stencil(read_second, x, runs, None, None, 1.6, emit, beside_z)

    def products(x, runs, total):
        pieces = []
        for begin, end in runs:
            inner = pl.ds(begin * LANES, (end - begin) * LANES)
            values = jnp.concatenate(
                [field[x, :, inner], field_s[x, :, inner], field_t[x - REACH, :, inner]], axis=0
            )
            coarse = values.astype(jnp.bfloat16)
            fine = (values - coarse.astype(f32)).astype(jnp.bfloat16)
            both = jnp.concatenate([coarse, fine], axis=0)
            split[x - REACH, :, pl.ds((begin - 1) * LANES, (end - begin) * LANES)] = both
            pieces.append(both)
        both = pieces[0] if len(pieces) == 1 else jnp.concatenate(pieces, axis=1)
        return total + lax.dot_general(
            both[:COLS], both, (((1,), (1,)), ((), ())), preferred_element_type=f32
        )

    def sweep(begin, end, total, first=None, second=None, third=None, inner=None):
        def step(x, total):
            if inner:
                total = products(x - 5, inner, total)
            if third:
                third_rows([(x - 4, third)])
            if second:
                second_rows([(x - 2, second)])
            if first:
                first_rows([(x, first)])
            return total

        return lax.fori_loop(begin, end, step, total)

    total = jnp.zeros((COLS, 2 * COLS), f32)
    f, s, t, p = ((1, 17),), ((2, 16),), ((3, 15),), ((3, 15),)
    sweep(4, 7, 0, f)
    sweep(7, 10, 0, f, s)
    sweep(10, 11, 0, f, s, t)
    total = sweep(11, 18, total, f, s, t, p)
    total = sweep(18, 19, total, None, s, t, p)
    total = sweep(19, 20, total, None, None, t, p)
    total = sweep(20, 21, total, None, None, None, p)

    for copy in copies + thirds:
        copy.wait_recv()

    whole, rim = ((0, 18),), ((0, 2), (16, 18))
    inner, inner_rim = ((1, 17),), ((1, 3), (15, 17))

    def rest_of_first(i, carry):
        rims = [(jnp.minimum(4 + 5 * i + j, CX + 1), rim) for j in range(5)]
        first_rows([(1 + i, whole), (CX + 2 + i, whole), *rims])
        return carry

    def rest_of_second(i, carry):
        rims = [(5 + 4 * i + j, rim) for j in range(4)]
        second_rows([(2 + i, whole), (CX + 1 + i, whole), *rims])
        return carry

    def rest_of_third(i):
        rims = [(jnp.minimum(6 + 4 * i + j, CX - 1), inner_rim) for j in range(4)]
        third_rows([(3 + i, inner), (CX + i, inner), *rims])

    def rest_of_products(i, total):
        total = products(3 + i, inner, total)
        total = products(CX + i, inner, total)
        for j in range(3):
            total = products(6 + 3 * i + j, inner_rim, total)
        return total

    def rest_of_both(i, total):
        total = rest_of_products(i - 1, total)
        rest_of_third(i)
        return total

    lax.fori_loop(0, REACH, rest_of_first, 0)
    lax.fori_loop(0, REACH, rest_of_second, 0)
    rest_of_third(0)
    total = lax.fori_loop(1, REACH, rest_of_both, total)
    total = rest_of_products(REACH - 1, total)
    total = products(CX - 1, inner_rim, total)
    store = pltpu.make_async_copy(split, cols, local_sem.at[2])
    store.start()
    mixed = total[:, COLS:]
    total = total[:, :COLS] + (mixed + mixed.T)
    empty = jnp.zeros((COLS // 2, HALF - COLS), f32)
    total = jnp.concatenate([total[: COLS // 2], empty, total[COLS // 2 :], empty], axis=1)

    for kind, (size, part) in enumerate(zip(GROUPS, (part0, part1, part2))):
        me = place(kind, gx, gy)
        part[me] = total
        sums = []
        for step in range(1, size):
            copy = pltpu.make_async_remote_copy(
                src_ref=part.at[me],
                dst_ref=part.at[me],
                send_sem=sum_send.at[kind, step],
                recv_sem=sum_recv.at[kind, size - step],
                device_id=partner(kind, gx, gy, step),
                device_id_type=MESH,
            )
            copy.start()
            sums.append(copy)
        for copy in sums:
            copy.wait()
        total = part[0]
        for i in range(1, size):
            total = total + part[i]
    gram[...] = total

    for copy in cond_copies + copies + thirds:
        copy.wait_send()
    store.wait()


def basis_kernel(cols, gram, basis, triangle, held, result, load_sem, store_sem):
    f32 = jnp.float32
    chunks = 8
    width = MERGED // chunks

    def part(i):
        lanes = pl.ds(pl.multiple_of(i * width, width), width)
        return pltpu.make_async_copy(cols.at[:, :, lanes], held.at[:, :, lanes], load_sem.at[i])

    def begin(i, carry):
        part(i).start()
        return carry

    lax.fori_loop(0, chunks, begin, 0)

    packed = gram[...]
    full = jnp.concatenate([packed, pltpu.roll(packed, HALF, 1)], axis=0)
    row = lax.broadcasted_iota(jnp.int32, (8, LANES), 0)
    lane = lax.broadcasted_iota(jnp.int32, (8, LANES), 1)
    count = COLS // 8
    matrix = []
    for i in range(count):
        unit = jnp.where(lane == row + (HALF + 8 * i), 1.0, 0.0)
        matrix.append(jnp.where(lane < COLS, full[8 * i : 8 * i + 8], unit))
    pivots = [jnp.ones((8, LANES), f32) for _ in range(count)]

    def across(v, k):
        return jnp.broadcast_to(v[:, k : k + 1], (8, LANES))

    def down(v, r):
        return jnp.broadcast_to(v[r : r + 1, :], (8, LANES))

    for k in range(0, COLS, 2):
        block, r = k // 8, k % 8
        near = {i: across(matrix[i], k) for i in range(block, count)}
        far = {i: across(matrix[i], k + 1) for i in range(block, count)}
        row_near = down(matrix[block], r)
        row_far = down(matrix[block], r + 1)
        p, q, o = down(near[block], r), down(far[block], r + 1), down(far[block], r)
        inverse_near = 1.0 / p
        inverse_far = p / (p * q - o * o)
        ratio = o * inverse_near
        row_far = row_far - ratio * row_near
        for i in range(block, count):
            first = near[i] * inverse_near
            second = (far[i] - first * o) * inverse_far
            if i == block:
                second = jnp.where(row > r + 1, second, 0.0)
                pivots[i] = jnp.where(row == r, p, pivots[i])
                pivots[i] = jnp.where(row == r + 1, q - ratio * o, pivots[i])
                first = jnp.where(row > r, first, 0.0)
            matrix[i] = matrix[i] - (first * row_near + second * row_far)
    size = math.sqrt(GX * CX * GY * MERGED)
    matrix = jnp.concatenate([m * lax.rsqrt(p) for m, p in zip(matrix, pivots)], axis=0)
    row = lax.broadcasted_iota(jnp.int32, (COLS, LANES), 0)
    lane = lax.broadcasted_iota(jnp.int32, (COLS, LANES), 1)
    upper = jnp.where((lane >= row) & (lane < COLS), matrix * (1.0 / size), 0.0)
    triangle[...] = upper[:, :COLS]
    inverse = pltpu.roll(matrix, HALF, 1)[:, :COLS] * size
    coarse = inverse.astype(jnp.bfloat16)
    fine = (inverse - coarse.astype(f32)).astype(jnp.bfloat16)
    weights = jnp.concatenate([coarse, coarse, fine], axis=1)

    per_chunk = width // LANES

    def send(h, t):
        return pltpu.make_async_copy(
            result.at[h, t].reshape(COLS, 8, LANES), basis.at[:, h, :, tile(t)], store_sem.at[h, t]
        )

    def solve(i, carry):
        part(i).wait()
        lanes = pl.ds(pl.multiple_of(i * width, width), width)
        for x in range(CX):
            both = held[x, :, lanes]
            stack = jnp.concatenate([both, both[:COLS]], axis=0)
            solved = jnp.dot(weights, stack, preferred_element_type=f32)
            for t in range(per_chunk):
                result[x // 8, i * per_chunk + t, pl.ds(x % 8, COLS, stride=8), :] = solved[
                    :, t * LANES : (t + 1) * LANES
                ]
        for h in range(2):
            for t in range(per_chunk):
                send(h, i * per_chunk + t).start()
        return carry

    lax.fori_loop(0, chunks, solve, 0)

    def finish(t, carry):
        for h in range(2):
            send(h, t).wait()
        return carry

    lax.fori_loop(0, TILES, finish, 0)


def per_device(initial_guess, conductivity, electrodes):
    f32 = jnp.float32
    any_space = pl.BlockSpec(memory_space=pltpu.HBM)
    vmem = pl.BlockSpec(memory_space=pltpu.VMEM)
    smem = pl.BlockSpec(memory_space=pltpu.SMEM)
    dma = pltpu.SemaphoreType.DMA
    cols, gram = pl.pallas_call(
        krylov_kernel,
        out_shape=(
            jax.ShapeDtypeStruct((CX, 2 * COLS, MERGED), jnp.bfloat16),
            jax.ShapeDtypeStruct((COLS // 2, LANES), f32),
        ),
        in_specs=[any_space, any_space, smem],
        out_specs=(any_space, vmem),
        scratch_shapes=[
            pltpu.VMEM((2, TILES, SRC * 8, LANES), f32),
            pltpu.VMEM((EXT_X, SRC, EXT), f32),
            pltpu.VMEM((EXT_X, SRC, EXT), f32),
            pltpu.VMEM((EXT_X, SRC, EXT), f32),
            pltpu.VMEM((CX, SRC, EXT), f32),
            pltpu.VMEM((CX + 16, EXT + 2 * LANES), f32),
            pltpu.VMEM((EXT_T, (CX + 16) * 8, LANES), f32),
            pltpu.VMEM((2 * LANES, 2 * LANES), jnp.bfloat16),
            pltpu.VMEM((2, 4, MERGED), f32),
            pltpu.VMEM((2, 4, MERGED), f32),
            pltpu.VMEM((2, CX // 2, SRC, LANES), f32),
            pltpu.VMEM((2, CX // 2, SRC, LANES), f32),
            pltpu.VMEM((CX, 2 * COLS, MERGED), jnp.bfloat16),
            pltpu.VMEM((GROUPS[0], COLS // 2, LANES), f32),
            pltpu.VMEM((GROUPS[1], COLS // 2, LANES), f32),
            pltpu.VMEM((GROUPS[2], COLS // 2, LANES), f32),
            dma((2, TILES)),
            dma((3,)),
            dma((8,)),
            dma((8,)),
            dma((8,)),
            dma((8,)),
            dma((2,)),
            dma((2,)),
            dma((3, 8)),
            dma((3, 8)),
        ],
        compiler_params=pltpu.CompilerParams(
            collective_id=0, has_side_effects=True, vmem_limit_bytes=60 * 2**20
        ),
        name="krylov",
    )(initial_guess.reshape(SRC, 2, 8, MERGED), conductivity, electrodes)
    basis, triangle = pl.pallas_call(
        basis_kernel,
        out_shape=(
            jax.ShapeDtypeStruct((COLS, 2, 8, MERGED), f32),
            jax.ShapeDtypeStruct((COLS, COLS), f32),
        ),
        in_specs=[any_space, vmem],
        out_specs=(any_space, vmem),
        scratch_shapes=[
            pltpu.VMEM((CX, 2 * COLS, MERGED), jnp.bfloat16),
            pltpu.VMEM((2, TILES, COLS * 8, LANES), f32),
            dma((8,)),
            dma((2, TILES)),
        ],
        compiler_params=pltpu.CompilerParams(vmem_limit_bytes=60 * 2**20),
        name="basis",
    )(cols, gram)
    return basis.reshape(COLS, CX, MERGED), triangle


def solution(mesh):
    return jax.shard_map(
        per_device,
        mesh=mesh,
        in_specs=(P(None, "gx", "gy"), P("gx", "gy"), P()),
        out_specs=(P(None, "gx", "gy"), P()),
        check_vma=False,
    )
```

```python
import functools
import math

import jax
import jax.numpy as jnp
from jax import lax
from jax.experimental import pallas as pl
from jax.experimental.pallas import tpu as pltpu
from jax.sharding import PartitionSpec as P

MESH = pl.DeviceIdType.MESH
NZ = 64
SHARE = 2
LANES = 128
HALF = 64
SRC = 16
COLS = 48
CX = 16
TILES = 16
REACH = 3
EXT_X = CX + 2 * REACH
SPARE = EXT_X + 1
EXT_T = TILES + 2
EXT = EXT_T * LANES
MERGED = TILES * LANES
GX, GY = 32, 8
MOVES = ((1, 0), (-1, 0), (0, 1), (0, -1), (1, 1), (1, -1), (-1, 1), (-1, -1))


def tile(t):
    if isinstance(t, int):
        return pl.ds(t * LANES, LANES)
    return pl.ds(pl.multiple_of(t * LANES, LANES), LANES)


def swap_halves(v):
    return pltpu.roll(v, HALF, 1)


def partner(kind, gx, gy, step):
    if kind == 0:
        base = (gx // 8) * 8
        return (base + lax.rem(gx - base + step, 8), gy)
    if kind == 1:
        return (lax.rem(gx + 8 * step, GX), gy)
    return (gx, lax.rem(gy + step, GY))


def place(kind, gx, gy):
    return (lax.rem(gx, 8), gx // 8, gy)[kind]


GROUPS = (8, 4, 8)


def krylov_kernel(
    guess,
    cond,
    electrodes,
    cols,
    gram,
    natural,
    start,
    field,
    field_s,
    field_t,
    cond_ext,
    coef,
    shifts,
    cond_out,
    cond_in,
    third_out,
    third_in,
    split,
    part0,
    part1,
    part2,
    guess_sem,
    local_sem,
    cond_send,
    cond_recv,
    send,
    recv,
    third_send_sem,
    third_recv_sem,
    sum_send,
    sum_recv,
):
    gx, gy = lax.axis_index("gx"), lax.axis_index("gy")
    f32 = jnp.float32

    def beside(move):
        dx, dy = move
        return (lax.rem(gx + dx + GX, GX), lax.rem(gy + dy + GY, GY))

    barrier = pltpu.get_barrier_semaphore()

    def greet(i, carry):
        i = i + jnp.where(i >= 4, 1, 0)
        move = (i // 3 - 1, lax.rem(i, 3) - 1)
        pl.semaphore_signal(barrier, inc=1, device_id=beside(move), device_id_type=MESH)
        return carry

    lax.fori_loop(0, len(MOVES), greet, 0)

    def load(half, t):
        return pltpu.make_async_copy(
            guess.at[:, half, :, tile(t)],
            natural.at[half, t].reshape(SRC, 8, LANES),
            guess_sem.at[half, t],
        )

    def each_load(act):
        def step(t, carry):
            for half in range(2):
                act(load(half, t))
            return carry

        lax.fori_loop(0, TILES, step, 0)

    load_cond = pltpu.make_async_copy(
        cond, cond_ext.at[pl.ds(8, CX), pl.ds(2 * LANES, MERGED)], local_sem.at[1]
    )
    load_cond.start()
    each_load(lambda copy: copy.start())
    for kind, size in enumerate(GROUPS):


        def greet_group(step, carry, kind=kind):
            pl.semaphore_signal(
                barrier, inc=1, device_id=partner(kind, gx, gy, step), device_id_type=MESH
            )
            return carry

        lax.fori_loop(1, size, greet_group, 0)

    third_in[:, CX // 2] = jnp.zeros((2, SRC, LANES), f32)
    for x in (0, EXT_X - 1):
        for t in (0, EXT_T - 1):
            start[x, :, tile(t)] = jnp.zeros((SRC, LANES), f32)
    for x in (0, 8 + CX):
        for t in (0, EXT_T + 1):
            cond_ext[pl.ds(x, 8), tile(t)] = jnp.zeros((8, LANES), f32)
        cond_ext[pl.ds(x, 8), pl.ds(2 * LANES, MERGED)] = jnp.zeros((8, MERGED), f32)
    load_cond.wait()
    for i, x in enumerate((8 + CX - 4, 8)):
        cond_out[i] = cond_ext[pl.ds(x, 4), pl.ds(2 * LANES, MERGED)]

    pl.semaphore_wait(barrier, len(MOVES) + sum(GROUPS) - len(GROUPS))

    cond_copies = []
    for i, (dx, dy) in enumerate(MOVES):
        if dx == 0:
            rows_from, rows_to = pl.ds(0, CX), pl.ds(8, CX)
        elif dx > 0:
            rows_from, rows_to = pl.ds(CX - 8, 8), pl.ds(0, 8)
        else:
            rows_from, rows_to = pl.ds(0, 8), pl.ds(8 + CX, 8)
        if dy == 0:
            lanes_from = lanes_to = pl.ds(0, MERGED)
        elif dx == 0:
            lanes_from = pl.ds(MERGED - 2 * LANES if dy > 0 else 0, 2 * LANES)
            lanes_to = pl.ds(0 if dy > 0 else (TILES + 2) * LANES, 2 * LANES)
        else:
            lanes_from = tile(TILES - 1 if dy > 0 else 0)
            lanes_to = tile(1 if dy > 0 else TILES + 2)
        source, target = cond.at[rows_from, lanes_from], cond_ext.at[rows_to, lanes_to]
        if dy == 0:
            side = 0 if dx > 0 else 1
            source, target = cond_out.at[side], cond_in.at[side]
        cond_copies.append(
            pltpu.make_async_remote_copy(
                src_ref=source,
                dst_ref=target,
                send_sem=cond_send.at[i],
                recv_sem=cond_recv.at[i],
                device_id=beside((dx, dy)),
                device_id_type=MESH,
            )
        )
    for copy in cond_copies:
        copy.start()

    each_load(lambda copy: copy.wait())

    copies = []
    for i, (dx, dy) in enumerate(MOVES):
        depth = REACH if dy == 0 else 2
        if dx == 0:
            x_from, x_to = pl.ds(REACH, CX), pl.ds(REACH, CX)
        elif dx > 0:
            x_from, x_to = pl.ds(REACH + CX - depth, depth), pl.ds(REACH - depth, depth)
        else:
            x_from, x_to = pl.ds(REACH, depth), pl.ds(REACH + CX, depth)
        if dy == 0:
            lanes_from = lanes_to = pl.ds(LANES, MERGED)
        else:
            lanes_from = tile(TILES if dy > 0 else 1)
            lanes_to = tile(0 if dy > 0 else TILES + 1)
        copies.append(
            pltpu.make_async_remote_copy(
                src_ref=start.at[x_from, :, lanes_from],
                dst_ref=start.at[x_to, :, lanes_to],
                send_sem=send.at[i],
                recv_sem=recv.at[i],
                device_id=beside((dx, dy)),
                device_id_type=MESH,
            )
        )
    thirds = [
        pltpu.make_async_remote_copy(
            src_ref=third_out.at[i],
            dst_ref=third_in.at[i, pl.ds(0, CX // 2)],
            send_sem=third_send_sem.at[i],
            recv_sem=third_recv_sem.at[i],
            device_id=beside(move),
            device_id_type=MESH,
        )
        for i, move in enumerate(((0, 1), (0, -1)))
    ]
    along_x = [copy for copy, (dx, dy) in zip(copies, MOVES) if dx != 0]
    along_y = [copy for copy, (dx, dy) in zip(copies, MOVES) if dx == 0]

    def lay_out(i, carry):
        @pl.when(i == 2 * REACH)
        def _():
            for copy in along_x:
                copy.start()

        x = jnp.where(i < REACH, i, jnp.where(i < 2 * REACH, i + CX - 2 * REACH, i - REACH))
        half, rest = x // 8, lax.rem(x, 8)
        for t in range(TILES):
            start[x + REACH, :, tile(t + 1)] = natural[half, t, pl.ds(rest, SRC, stride=8), :]
        return carry

    lax.fori_loop(0, CX, lay_out, 0)
    lane = lax.broadcasted_iota(jnp.int32, (SRC, LANES), 1)
    low = lane < HALF

    def pack_third(x, carry):
        near, far = REACH + x, REACH + CX // 2 + x
        third_out[0, x] = jnp.where(
            low, swap_halves(start[near, :, tile(TILES - 1)]), start[far, :, tile(TILES - 1)]
        )
        third_out[1, x] = jnp.where(
            low, start[far, :, tile(2)], swap_halves(start[near, :, tile(2)])
        )
        return carry

    lax.fori_loop(0, CX // 2, pack_third, 0)

    for copy in along_y + thirds:
        copy.start()

    for copy in cond_copies:
        copy.wait()
    for i, x in enumerate((4, 8 + CX)):
        cond_ext[pl.ds(x, 4), pl.ds(2 * LANES, MERGED)] = cond_in[i]
    row = lax.broadcasted_iota(jnp.int32, (CX + 16, LANES), 0)
    lane_c = lax.broadcasted_iota(jnp.int32, (CX + 16, LANES), 1)
    first_x, last_x = gx == 0, gx == GX - 1
    row_from = jnp.where(first_x, 8, 0)
    row_to = jnp.where(last_x, 8 + CX, 16 + CX)
    inside_x = (row >= row_from) & (row < row_to)
    tile_from = jnp.where(gy == 0, 2, 0)
    tile_to = jnp.where(gy == GY - 1, TILES + 2, TILES + 4)
    z = lax.rem(lane_c, HALF)
    low_c = lane_c < HALF

    def couplings(t, carry):
        def load(place):
            row_end = jnp.where((place >= tile_from) & (place < tile_to), row_to, 0)
            return jnp.where(inside_x & (row < row_end), cond_ext[:, tile(place)], 0.0)

        here = load(t + 1)
        below, above = load(t), load(t + 2)
        swapped = swap_halves(here)
        outer = jnp.where(low_c, swap_halves(below), swap_halves(above))
        z_down = jnp.where(z == 0, 0.0, pltpu.roll(here, 1, 1))
        z_up = jnp.where(z == HALF - 1, 0.0, pltpu.roll(here, LANES - 1, 1))
        x_down = pltpu.roll(here, 1, 0)
        x_up = pltpu.roll(here, CX + 15, 0)
        total = 6.0 * here
        for k, there in enumerate((x_down, x_up, swapped, outer, z_down, z_up)):
            total = total + there
            face = jnp.where((here > 0.0) & (there > 0.0), -0.5 * (here + there), 0.0)
            coef[t, pl.ds(k, CX + 16, stride=8), :] = face
        coef[t, pl.ds(6, CX + 16, stride=8), :] = jnp.where(here > 0.0, 0.5 * total, 0.0)
        return carry

    lax.fori_loop(0, EXT_T, couplings, 0)

    inward = lax.rem(lax.broadcasted_iota(jnp.int32, (2 * LANES, 2 * LANES), 0), LANES)
    outward = lax.broadcasted_iota(jnp.int32, (2 * LANES, 2 * LANES), 1)
    outward = jnp.where(outward < LANES, outward - 1, outward - (LANES - 1))
    shifts[...] = jnp.where(inward == outward, 1.0, 0.0).astype(jnp.bfloat16)

    def along_z(values):
        values = jnp.concatenate(values, axis=0)
        coarse = values.astype(jnp.bfloat16)
        fine = (values - coarse.astype(f32)).astype(jnp.bfloat16)
        both = jnp.concatenate([coarse, fine], axis=1)
        return jnp.dot(both, shifts[...], preferred_element_type=f32)

    def around(read, jobs):
        places = [
            (x, t)
            for x, runs in jobs
            for begin, end in runs
            for t in range(begin, end)
            if t % SHARE == 1
        ]
        both = along_z([read(x, t) for x, t in places])
        found = []
        for x, runs in jobs:
            row = {}
            for begin, end in runs:
                for t in range(begin, end):
                    if t % SHARE == 1:
                        row[t] = both[:SRC, :LANES], both[:SRC, LANES:]
                        both = both[SRC:]
            found.append(row)
        return found

    def stencil(read, x, runs, left, right, shift, emit, beside_z):
        base = pl.multiple_of((x + 8 - REACH) * 8, 8)
        for begin, end in runs:
            value = read(x, begin)
            turned = swap_halves(value)
            if begin > 0:
                before = swap_halves(read(x, begin - 1))
            else:
                before = turned if left is None else left
            for t in range(begin, end):
                c = [
                    jnp.broadcast_to(coef[t, pl.ds(base + k, 1), :], (SRC, LANES))
                    for k in range(7)
                ]
                if t == EXT_T - 1:
                    following, after = None, turned if right is None else right
                else:
                    following = read(x, t + 1)
                    after = swap_halves(following)
                diagonal = c[6] if shift == 0.0 else c[6] - shift
                if t in beside_z:
                    z_down, z_up = beside_z[t]
                else:
                    z_down, z_up = pltpu.roll(value, 1, 1), pltpu.roll(value, LANES - 1, 1)
                near = diagonal * value + c[2] * turned
                across = c[0] * read(x - 1, t) + c[1] * read(x + 1, t)
                along = c[4] * z_down + c[5] * z_up
                total = (near + across) + (along + c[3] * jnp.where(low, before, after))
                emit(t, total)
                value, before, turned = following, turned, after

    spot = jnp.zeros((SRC, LANES), jnp.int32)
    source = lax.broadcasted_iota(jnp.int32, (SRC, LANES), 0)
    for k in range(SRC):
        spot = jnp.where(source == k, electrodes[k], spot)
    spot = spot - lane

    def outer_thirds(x):
        p = x - REACH
        centre = (p >= 0) & (p < CX)
        held = jnp.where(centre, lax.rem(p + CX // 2, CX // 2), CX // 2)
        far = p >= CX // 2
        left = third_in[0, held]
        right = third_in[1, held]
        left = jnp.where(far, swap_halves(left), left)
        right = jnp.where(far, swap_halves(right), right)
        return left, right

    def read_start(x, t):
        return start[x, :, tile(t)]

    def first_rows(jobs):
        for (x, runs), beside_z in zip(jobs, around(read_start, jobs)):
            first_row(x, runs, beside_z)

    def first_row(x, runs, beside_z):
        cell_x = gx * CX + x - REACH
        inside = (cell_x >= 0) & (cell_x < GX * CX)
        origin = (cell_x * (GY * TILES) + gy * TILES - 1) * LANES
        left = right = None
        if runs[0][0] == 0:
            left, right = outer_thirds(x)

        def emit(t, total):
            ok = inside
            if t == 0:
                ok = ok & (gy > 0)
            if t == EXT_T - 1:
                ok = ok & (gy < GY - 1)
            cell = jnp.where(ok, origin + t * LANES, -(2**30))
            field[x, :, tile(t)] = jnp.where(spot == cell, 20.0, 0.0) - total

        stencil(read_start, x, runs, left, right, 0.0, emit, beside_z)


    def read_first(x, t):
        return field[x, :, tile(t)]

    def second_rows(jobs):
        for (x, runs), beside_z in zip(jobs, around(read_first, jobs)):
            second_row(x, runs, beside_z)

    def second_row(x, runs, beside_z):
        def emit(t, total):
            field_s[x, :, tile(t)] = total

        stencil(read_first, x, runs, None, None, 0.8, emit, beside_z)

    def read_second(x, t):
        return field_s[x, :, tile(t)]

    def third_rows(jobs):
        for (x, runs), beside_z in zip(jobs, around(read_second, jobs)):
            third_row(x, runs, beside_z)

    def third_row(x, runs, beside_z):
        def emit(t, total):
            field_t[x - REACH, :, tile(t)] = total

        stencil(read_second, x, runs, None, None, 1.6, emit, beside_z)

    def products(x, runs):
        pieces = []
        for begin, end in runs:
            inner = pl.ds(begin * LANES, (end - begin) * LANES)
            values = jnp.concatenate(
                [field[x, :, inner], field_s[x, :, inner], field_t[x - REACH, :, inner]], axis=0
            )
            coarse = values.astype(jnp.bfloat16)
            fine = (values - coarse.astype(f32)).astype(jnp.bfloat16)
            both = jnp.concatenate([coarse, fine], axis=0)
            split[x - REACH, :, pl.ds((begin - 1) * LANES, (end - begin) * LANES)] = both
            pieces.append(both)
        both = pieces[0] if len(pieces) == 1 else jnp.concatenate(pieces, axis=1)
        return lax.dot_general(
            both[:COLS], both, (((1,), (1,)), ((), ())), preferred_element_type=f32
        )

    whole, inner = ((0, EXT_T),), ((1, TILES + 1),)

    def turn(x, total):
        @pl.when(x == 1)
        def _():
            for copy in copies + thirds:
                copy.wait()

        def row(shift, first, last):
            return jnp.minimum(jnp.maximum(x - shift, first), last)

        own = products(row(5, REACH, REACH + CX - 1), inner)
        total = jnp.where(x >= 5 + REACH, total + own, 0.0)
        third_rows([(row(4, REACH, REACH + CX - 1), inner)])
        second_rows([(row(2, 2, EXT_X - 3), whole)])
        first_rows([(jnp.where(x == 0, SPARE, row(0, 1, EXT_X - 2)), whole)])
        return total

    total = lax.fori_loop(0, CX + 8, turn, jnp.zeros((COLS, 2 * COLS), f32))
    store = pltpu.make_async_copy(split, cols, local_sem.at[2])
    store.start()
    mixed = total[:, COLS:]
    total = total[:, :COLS] + (mixed + mixed.T)
    empty = jnp.zeros((COLS // 2, HALF - COLS), f32)
    total = jnp.concatenate([total[: COLS // 2], empty, total[COLS // 2 :], empty], axis=1)

    for kind, (size, part) in enumerate(zip(GROUPS, (part0, part1, part2))):
        me = place(kind, gx, gy)
        part[me] = total

        def share(step, kind=kind, size=size, part=part, me=me):
            return pltpu.make_async_remote_copy(
                src_ref=part.at[me],
                dst_ref=part.at[me],
                send_sem=sum_send.at[kind, step],
                recv_sem=sum_recv.at[kind, size - step],
                device_id=partner(kind, gx, gy, step),
                device_id_type=MESH,
            )

        def begin_share(step, carry, share=share):
            share(step).start()
            return carry

        def end_share(step, carry, share=share):
            share(step).wait()
            return carry

        lax.fori_loop(1, size, begin_share, 0)
        lax.fori_loop(1, size, end_share, 0)
        total = part[0]
        for i in range(1, size):
            total = total + part[i]
    gram[...] = total

    store.wait()


def basis_kernel(cols, gram, basis, triangle, held, result, load_sem, store_sem):
    f32 = jnp.float32
    chunks = 8
    width = MERGED // chunks

    def part(i):
        lanes = pl.ds(pl.multiple_of(i * width, width), width)
        return pltpu.make_async_copy(cols.at[:, :, lanes], held.at[:, :, lanes], load_sem.at[i])

    def begin(i, carry):
        part(i).start()
        return carry

    lax.fori_loop(0, chunks, begin, 0)

    packed = gram[...]
    full = jnp.concatenate([packed, pltpu.roll(packed, HALF, 1)], axis=0)
    row = lax.broadcasted_iota(jnp.int32, (8, LANES), 0)
    lane = lax.broadcasted_iota(jnp.int32, (8, LANES), 1)
    count = COLS // 8
    matrix = []
    for i in range(count):
        unit = jnp.where(lane == row + (HALF + 8 * i), 1.0, 0.0)
        matrix.append(jnp.where(lane < COLS, full[8 * i : 8 * i + 8], unit))

    def across(v, k):
        return jnp.broadcast_to(v[:, k : k + 1], (8, LANES))

    def down(v, r):
        return jnp.broadcast_to(v[r : r + 1, :], (8, LANES))

    def eliminate(turn, carry):
        matrix = list(carry)
        for r in range(0, 8, 2):
            near = [across(m, r) for m in matrix]
            far = [across(m, r + 1) for m in matrix]
            row_near = down(matrix[0], r)
            row_far = down(matrix[0], r + 1)
            p, q, o = down(near[0], r), down(far[0], r + 1), down(far[0], r)
            inverse_near = 1.0 / p
            inverse_far = p / (p * q - o * o)
            ratio = o * inverse_near
            row_far = row_far - ratio * row_near
            for i in range(count):
                first = near[i] * inverse_near
                second = (far[i] - first * o) * inverse_far
                if i == 0:
                    first = jnp.where(row > r, first, 0.0)
                    second = jnp.where(row > r + 1, second, 0.0)
                change = first * row_near + second * row_far
                if i > 0:
                    change = jnp.where(turn < count - i, change, 0.0)
                matrix[i] = matrix[i] - change
        return tuple(pltpu.roll(m, LANES - 8, 1) for m in matrix[1:] + matrix[:1])

    matrix = lax.fori_loop(0, count, eliminate, tuple(matrix))
    size = math.sqrt(GX * CX * GY * MERGED)
    matrix = pltpu.roll(jnp.concatenate(matrix, axis=0), COLS, 1)
    row = lax.broadcasted_iota(jnp.int32, (COLS, LANES), 0)
    lane = lax.broadcasted_iota(jnp.int32, (COLS, LANES), 1)
    pivots = jnp.sum(jnp.where(lane == row, matrix, 0.0), axis=1, keepdims=True)
    matrix = matrix * lax.rsqrt(pivots)
    upper = jnp.where((lane >= row) & (lane < COLS), matrix * (1.0 / size), 0.0)
    triangle[...] = upper[:, :COLS]
    inverse = pltpu.roll(matrix, HALF, 1)[:, :COLS] * size
    coarse = inverse.astype(jnp.bfloat16)
    fine = (inverse - coarse.astype(f32)).astype(jnp.bfloat16)
    weights = jnp.concatenate([coarse, coarse, fine], axis=1)

    per_chunk = width // LANES

    def send(h, t):
        return pltpu.make_async_copy(
            result.at[h, t].reshape(COLS, 8, LANES), basis.at[:, h, :, tile(t)], store_sem.at[h, t]
        )

    def solve(i, carry):
        part(i).wait()
        lanes = pl.ds(pl.multiple_of(i * width, width), width)

        def half(h, carry):
            for rest in range(8):
                both = held[h * 8 + rest, :, lanes]
                stack = jnp.concatenate([both, both[:COLS]], axis=0)
                solved = jnp.dot(weights, stack, preferred_element_type=f32)
                for t in range(per_chunk):
                    result[h, i * per_chunk + t, pl.ds(rest, COLS, stride=8), :] = solved[
                        :, t * LANES : (t + 1) * LANES
                    ]
            for t in range(per_chunk):
                send(h, i * per_chunk + t).start()
            return carry

        return lax.fori_loop(0, 2, half, carry)

    lax.fori_loop(0, chunks, solve, 0)

    def finish(t, carry):
        for h in range(2):
            send(h, t).wait()
        return carry

    lax.fori_loop(0, TILES, finish, 0)


def per_device(initial_guess, conductivity, electrodes):
    f32 = jnp.float32
    any_space = pl.BlockSpec(memory_space=pltpu.HBM)
    vmem = pl.BlockSpec(memory_space=pltpu.VMEM)
    smem = pl.BlockSpec(memory_space=pltpu.SMEM)
    dma = pltpu.SemaphoreType.DMA
    cols, gram = pl.pallas_call(
        krylov_kernel,
        out_shape=(
            jax.ShapeDtypeStruct((CX, 2 * COLS, MERGED), jnp.bfloat16),
            jax.ShapeDtypeStruct((COLS // 2, LANES), f32),
        ),
        in_specs=[any_space, any_space, smem],
        out_specs=(any_space, vmem),
        scratch_shapes=[
            pltpu.VMEM((2, TILES, SRC * 8, LANES), f32),
            pltpu.VMEM((EXT_X + 3, SRC, EXT), f32),
            pltpu.VMEM((EXT_X + 3, SRC, EXT), f32),
            pltpu.VMEM((EXT_X + 3, SRC, EXT), f32),
            pltpu.VMEM((CX, SRC, EXT), f32),
            pltpu.VMEM((CX + 16, EXT + 2 * LANES), f32),
            pltpu.VMEM((EXT_T, (CX + 16) * 8, LANES), f32),
            pltpu.VMEM((2 * LANES, 2 * LANES), jnp.bfloat16),
            pltpu.VMEM((2, 4, MERGED), f32),
            pltpu.VMEM((2, 4, MERGED), f32),
            pltpu.VMEM((2, CX // 2, SRC, LANES), f32),
            pltpu.VMEM((2, CX // 2 + 1, SRC, LANES), f32),
            pltpu.VMEM((CX, 2 * COLS, MERGED), jnp.bfloat16),
            pltpu.VMEM((GROUPS[0], COLS // 2, LANES), f32),
            pltpu.VMEM((GROUPS[1], COLS // 2, LANES), f32),
            pltpu.VMEM((GROUPS[2], COLS // 2, LANES), f32),
            dma((2, TILES)),
            dma((3,)),
            dma((8,)),
            dma((8,)),
            dma((8,)),
            dma((8,)),
            dma((2,)),
            dma((2,)),
            dma((3, 8)),
            dma((3, 8)),
        ],
        compiler_params=pltpu.CompilerParams(
            collective_id=0, has_side_effects=True, vmem_limit_bytes=60 * 2**20
        ),
        name="krylov",
    )(initial_guess.reshape(SRC, 2, 8, MERGED), conductivity, electrodes)
    basis, triangle = pl.pallas_call(
        basis_kernel,
        out_shape=(
            jax.ShapeDtypeStruct((COLS, 2, 8, MERGED), f32),
            jax.ShapeDtypeStruct((COLS, COLS), f32),
        ),
        in_specs=[any_space, vmem],
        out_specs=(any_space, vmem),
        scratch_shapes=[
            pltpu.VMEM((CX, 2 * COLS, MERGED), jnp.bfloat16),
            pltpu.VMEM((2, TILES, COLS * 8, LANES), f32),
            dma((8,)),
            dma((2, TILES)),
        ],
        compiler_params=pltpu.CompilerParams(vmem_limit_bytes=60 * 2**20),
        name="basis",
    )(cols, gram)
    return basis.reshape(COLS, CX, MERGED), triangle


def solution(mesh):
    return jax.shard_map(
        per_device,
        mesh=mesh,
        in_specs=(P(None, "gx", "gy"), P("gx", "gy"), P()),
        out_specs=(P(None, "gx", "gy"), P()),
        check_vma=False,
    )
```

```python
import functools
import math

import jax
import jax.numpy as jnp
from jax import lax
from jax.experimental import pallas as pl
from jax.experimental.pallas import tpu as pltpu
from jax.sharding import PartitionSpec as P

MESH = pl.DeviceIdType.MESH
NZ = 64
SHARE = 2
LANES = 128
HALF = 64
SRC = 16
COLS = 48
CX = 16
TILES = 16
REACH = 3
EXT_X = CX + 2 * REACH
EXT_T = TILES + 2
EXT = EXT_T * LANES
MERGED = TILES * LANES
GX, GY = 32, 8
MOVES = ((1, 0), (-1, 0), (0, 1), (0, -1), (1, 1), (1, -1), (-1, 1), (-1, -1))


def tile(t):
    if isinstance(t, int):
        return pl.ds(t * LANES, LANES)
    return pl.ds(pl.multiple_of(t * LANES, LANES), LANES)


def swap_halves(v):
    return pltpu.roll(v, HALF, 1)


def partner(kind, gx, gy, step):
    if kind == 0:
        base = (gx // 8) * 8
        return (base + lax.rem(gx - base + step, 8), gy)
    if kind == 1:
        return (lax.rem(gx + 8 * step, GX), gy)
    return (gx, lax.rem(gy + step, GY))


def place(kind, gx, gy):
    return (lax.rem(gx, 8), gx // 8, gy)[kind]


GROUPS = (8, 4, 8)


def krylov_kernel(
    guess,
    cond,
    electrodes,
    cols,
    gram,
    start,
    field,
    field_s,
    field_t,
    cond_ext,
    coef,
    shifts,
    cond_out,
    cond_in,
    third_out,
    third_in,
    split,
    part0,
    part1,
    part2,
    guess_sem,
    local_sem,
    cond_send,
    cond_recv,
    send,
    recv,
    third_send_sem,
    third_recv_sem,
    sum_send,
    sum_recv,
):
    gx, gy = lax.axis_index("gx"), lax.axis_index("gy")
    f32 = jnp.float32

    def beside(move):
        dx, dy = move
        return (lax.rem(gx + dx + GX, GX), lax.rem(gy + dy + GY, GY))

    barrier = pltpu.get_barrier_semaphore()
    for move in MOVES:
        pl.semaphore_signal(barrier, inc=1, device_id=beside(move), device_id_type=MESH)

    def load(x):
        return pltpu.make_async_copy(
            guess.at[:, x, :], start.at[REACH + x, :, pl.ds(LANES, MERGED)], guess_sem.at[x]
        )

    faces = (*range(REACH), *range(CX - REACH, CX))
    between = tuple(range(REACH, CX - REACH))
    load_cond = pltpu.make_async_copy(
        cond, cond_ext.at[pl.ds(8, CX), pl.ds(2 * LANES, MERGED)], local_sem.at[1]
    )
    load_cond.start()
    for x in faces + between:
        load(x).start()
    for kind, size in enumerate(GROUPS):
        for step in range(1, size):
            pl.semaphore_signal(
                barrier, inc=1, device_id=partner(kind, gx, gy, step), device_id_type=MESH
            )

    for x in (0, EXT_X - 1):
        for t in (0, EXT_T - 1):
            start[x, :, tile(t)] = jnp.zeros((SRC, LANES), f32)
    for x in (0, 8 + CX):
        for t in (0, EXT_T + 1):
            cond_ext[pl.ds(x, 8), tile(t)] = jnp.zeros((8, LANES), f32)
        cond_ext[pl.ds(x, 8), pl.ds(2 * LANES, MERGED)] = jnp.zeros((8, MERGED), f32)
    load_cond.wait()
    for i, x in enumerate((8 + CX - 4, 8)):
        cond_out[i] = cond_ext[pl.ds(x, 4), pl.ds(2 * LANES, MERGED)]

    pl.semaphore_wait(barrier, len(MOVES) + sum(GROUPS) - len(GROUPS))

    cond_copies = []
    for i, (dx, dy) in enumerate(MOVES):
        if dx == 0:
            rows_from, rows_to = pl.ds(0, CX), pl.ds(8, CX)
        elif dx > 0:
            rows_from, rows_to = pl.ds(CX - 8, 8), pl.ds(0, 8)
        else:
            rows_from, rows_to = pl.ds(0, 8), pl.ds(8 + CX, 8)
        if dy == 0:
            lanes_from = lanes_to = pl.ds(0, MERGED)
        elif dx == 0:
            lanes_from = pl.ds(MERGED - 2 * LANES if dy > 0 else 0, 2 * LANES)
            lanes_to = pl.ds(0 if dy > 0 else (TILES + 2) * LANES, 2 * LANES)
        else:
            lanes_from = tile(TILES - 1 if dy > 0 else 0)
            lanes_to = tile(1 if dy > 0 else TILES + 2)
        source, target = cond.at[rows_from, lanes_from], cond_ext.at[rows_to, lanes_to]
        if dy == 0:
            side = 0 if dx > 0 else 1
            source, target = cond_out.at[side], cond_in.at[side]
        cond_copies.append(
            pltpu.make_async_remote_copy(
                src_ref=source,
                dst_ref=target,
                send_sem=cond_send.at[i],
                recv_sem=cond_recv.at[i],
                device_id=beside((dx, dy)),
                device_id_type=MESH,
            )
        )
    for copy in cond_copies:
        copy.start()

    for x in faces:
        load(x).wait()

    copies = []
    for i, (dx, dy) in enumerate(MOVES):
        depth = REACH if dy == 0 else 2
        if dx == 0:
            x_from, x_to = pl.ds(REACH, CX), pl.ds(REACH, CX)
        elif dx > 0:
            x_from, x_to = pl.ds(REACH + CX - depth, depth), pl.ds(REACH - depth, depth)
        else:
            x_from, x_to = pl.ds(REACH, depth), pl.ds(REACH + CX, depth)
        if dy == 0:
            lanes_from = lanes_to = pl.ds(LANES, MERGED)
        else:
            lanes_from = tile(TILES if dy > 0 else 1)
            lanes_to = tile(0 if dy > 0 else TILES + 1)
        copies.append(
            pltpu.make_async_remote_copy(
                src_ref=start.at[x_from, :, lanes_from],
                dst_ref=start.at[x_to, :, lanes_to],
                send_sem=send.at[i],
                recv_sem=recv.at[i],
                device_id=beside((dx, dy)),
                device_id_type=MESH,
            )
        )
    thirds = [
        pltpu.make_async_remote_copy(
            src_ref=third_out.at[i],
            dst_ref=third_in.at[i],
            send_sem=third_send_sem.at[i],
            recv_sem=third_recv_sem.at[i],
            device_id=beside(move),
            device_id_type=MESH,
        )
        for i, move in enumerate(((0, 1), (0, -1)))
    ]
    along_x = [copy for copy, (dx, dy) in zip(copies, MOVES) if dx != 0]
    along_y = [copy for copy, (dx, dy) in zip(copies, MOVES) if dx == 0]
    for copy in along_x:
        copy.start()

    for x in between:
        load(x).wait()
    lane = lax.broadcasted_iota(jnp.int32, (SRC, LANES), 1)
    low = lane < HALF

    def pack_third(x, carry):
        near, far = REACH + x, REACH + CX // 2 + x
        third_out[0, x] = jnp.where(
            low, swap_halves(start[near, :, tile(TILES - 1)]), start[far, :, tile(TILES - 1)]
        )
        third_out[1, x] = jnp.where(
            low, start[far, :, tile(2)], swap_halves(start[near, :, tile(2)])
        )
        return carry

    lax.fori_loop(0, CX // 2, pack_third, 0)

    for copy in along_y + thirds:
        copy.start()

    for copy in cond_copies:
        copy.wait_recv()
    for i, x in enumerate((4, 8 + CX)):
        cond_ext[pl.ds(x, 4), pl.ds(2 * LANES, MERGED)] = cond_in[i]
    row = lax.broadcasted_iota(jnp.int32, (CX + 16, LANES), 0)
    lane_c = lax.broadcasted_iota(jnp.int32, (CX + 16, LANES), 1)
    first_x, last_x = gx == 0, gx == GX - 1
    row_from = jnp.where(first_x, 8, 0)
    row_to = jnp.where(last_x, 8 + CX, 16 + CX)
    inside_x = (row >= row_from) & (row < row_to)
    tile_from = jnp.where(gy == 0, 2, 0)
    tile_to = jnp.where(gy == GY - 1, TILES + 2, TILES + 4)
    z = lax.rem(lane_c, HALF)
    low_c = lane_c < HALF

    def couplings(t, carry):
        def load(place):
            row_end = jnp.where((place >= tile_from) & (place < tile_to), row_to, 0)
            return jnp.where(inside_x & (row < row_end), cond_ext[:, tile(place)], 0.0)

        here = load(t + 1)
        below, above = load(t), load(t + 2)
        swapped = swap_halves(here)
        outer = jnp.where(low_c, swap_halves(below), swap_halves(above))
        z_down = jnp.where(z == 0, 0.0, pltpu.roll(here, 1, 1))
        z_up = jnp.where(z == HALF - 1, 0.0, pltpu.roll(here, LANES - 1, 1))
        x_down = pltpu.roll(here, 1, 0)
        x_up = pltpu.roll(here, CX + 15, 0)
        total = 6.0 * here
        for k, there in enumerate((x_down, x_up, swapped, outer, z_down, z_up)):
            total = total + there
            face = jnp.where((here > 0.0) & (there > 0.0), -0.5 * (here + there), 0.0)
            coef[t, pl.ds(k, CX + 16, stride=8), :] = face
        coef[t, pl.ds(6, CX + 16, stride=8), :] = jnp.where(here > 0.0, 0.5 * total, 0.0)
        return carry

    lax.fori_loop(0, EXT_T, couplings, 0)

    inward = lax.rem(lax.broadcasted_iota(jnp.int32, (2 * LANES, 2 * LANES), 0), LANES)
    outward = lax.broadcasted_iota(jnp.int32, (2 * LANES, 2 * LANES), 1)
    outward = jnp.where(outward < LANES, outward - 1, outward - (LANES - 1))
    shifts[...] = jnp.where(inward == outward, 1.0, 0.0).astype(jnp.bfloat16)

    def along_z(values):
        values = jnp.concatenate(values, axis=0)
        coarse = values.astype(jnp.bfloat16)
        fine = (values - coarse.astype(f32)).astype(jnp.bfloat16)
        both = jnp.concatenate([coarse, fine], axis=1)
        return jnp.dot(both, shifts[...], preferred_element_type=f32)

    def around(read, jobs):
        places = [
            (x, t)
            for x, runs in jobs
            for begin, end in runs
            for t in range(begin, end)
            if t % SHARE == 1
        ]
        both = along_z([read(x, t) for x, t in places])
        found = []
        for x, runs in jobs:
            row = {}
            for begin, end in runs:
                for t in range(begin, end):
                    if t % SHARE == 1:
                        row[t] = both[:SRC, :LANES], both[:SRC, LANES:]
                        both = both[SRC:]
            found.append(row)
        return found

    def stencil(read, x, runs, left, right, shift, emit, beside_z, closed=False):
        base = pl.multiple_of((x + 8 - REACH) * 8, 8)
        for begin, end in runs:
            value = read(x, begin)
            turned = swap_halves(value)
            if closed:
                before = turned
            elif begin > 0:
                before = swap_halves(read(x, begin - 1))
            else:
                before = turned if left is None else left
            for t in range(begin, end):
                c = [
                    jnp.broadcast_to(coef[t, pl.ds(base + k, 1), :], (SRC, LANES))
                    for k in range(7)
                ]
                if closed and t == end - 1:
                    following, after = None, turned
                elif t == EXT_T - 1:
                    following, after = None, turned if right is None else right
                else:
                    following = read(x, t + 1)
                    after = swap_halves(following)
                diagonal = c[6] if shift == 0.0 else c[6] - shift
                if t in beside_z:
                    z_down, z_up = beside_z[t]
                else:
                    z_down, z_up = pltpu.roll(value, 1, 1), pltpu.roll(value, LANES - 1, 1)
                near = diagonal * value + c[2] * turned
                across = c[0] * read(x - 1, t) + c[1] * read(x + 1, t)
                along = c[4] * z_down + c[5] * z_up
                total = (near + across) + (along + c[3] * jnp.where(low, before, after))
                emit(t, total)
                value, before, turned = following, turned, after

    spot = jnp.zeros((SRC, LANES), jnp.int32)
    source = lax.broadcasted_iota(jnp.int32, (SRC, LANES), 0)
    for k in range(SRC):
        spot = jnp.where(source == k, electrodes[k], spot)
    spot = spot - lane

    def outer_thirds(x):
        p = x - REACH
        centre = (p >= 0) & (p < CX)
        held = jnp.where(centre, lax.rem(p + CX // 2, CX // 2), 0)
        far = p >= CX // 2
        left = third_in[0, held]
        right = third_in[1, held]
        left = jnp.where(far, swap_halves(left), left)
        right = jnp.where(far, swap_halves(right), right)
        return left, right

    def read_start(x, t):
        return start[x, :, tile(t)]

    def first_rows(jobs):
        for (x, runs), beside_z in zip(jobs, around(read_start, jobs)):
            first_row(x, runs, beside_z)

    def first_row(x, runs, beside_z):
        cell_x = gx * CX + x - REACH
        inside = (cell_x >= 0) & (cell_x < GX * CX)
        origin = (cell_x * (GY * TILES) + gy * TILES - 1) * LANES
        left = right = None
        if runs[0][0] == 0:
            left, right = outer_thirds(x)

        def emit(t, total):
            ok = inside
            if t == 0:
                ok = ok & (gy > 0)
            if t == EXT_T - 1:
                ok = ok & (gy < GY - 1)
            cell = jnp.where(ok, origin + t * LANES, -(2**30))
            field[x, :, tile(t)] = jnp.where(spot == cell, 20.0, 0.0) - total

        closed = runs[0][0] == 1
        stencil(read_start, x, runs, left, right, 0.0, emit, beside_z, closed)


    def read_first(x, t):
        return field[x, :, tile(t)]

    def second_rows(jobs):
        for (x, runs), beside_z in zip(jobs, around(read_first, jobs)):
            second_row(x, runs, beside_z)

    def second_row(x, runs, beside_z):
        def emit(t, total):
            field_s[x, :, tile(t)] = total

        stencil(read_first, x, runs, None, None, 0.8, emit, beside_z)

    def read_second(x, t):
        return field_s[x, :, tile(t)]

    def third_rows(jobs):
        for (x, runs), beside_z in zip(jobs, around(read_second, jobs)):
            third_row(x, runs, beside_z)

    def third_row(x, runs, beside_z):
        def emit(t, total):
            field_t[x - REACH, :, tile(t)] = total

        stencil(read_second, x, runs, None, None, 1.6, emit, beside_z)

    def products(x, runs, total):
        pieces = []
        for begin, end in runs:
            inner = pl.ds(begin * LANES, (end - begin) * LANES)
            values = jnp.concatenate(
                [field[x, :, inner], field_s[x, :, inner], field_t[x - REACH, :, inner]], axis=0
            )
            coarse = values.astype(jnp.bfloat16)
            fine = (values - coarse.astype(f32)).astype(jnp.bfloat16)
            both = jnp.concatenate([coarse, fine], axis=0)
            split[x - REACH, :, pl.ds((begin - 1) * LANES, (end - begin) * LANES)] = both
            pieces.append(both)
        both = pieces[0] if len(pieces) == 1 else jnp.concatenate(pieces, axis=1)
        return total + lax.dot_general(
            both[:COLS], both, (((1,), (1,)), ((), ())), preferred_element_type=f32
        )

    def sweep(begin, end, total, first=None, second=None, third=None, inner=None):
        def step(x, total):
            if inner:
                total = products(x - 5, inner, total)
            if third:
                third_rows([(x - 4, third)])
            if second:
                second_rows([(x - 2, second)])
            if first:
                first_rows([(x, first)])
            return total

        return lax.fori_loop(begin, end, step, total)

    total = jnp.zeros((COLS, 2 * COLS), f32)
    f, s, t, p = ((1, 17),), ((2, 16),), ((3, 15),), ((3, 15),)
    sweep(4, 7, 0, f)
    sweep(7, 10, 0, f, s)
    sweep(10, 11, 0, f, s, t)
    total = sweep(11, 18, total, f, s, t, p)
    total = sweep(18, 19, total, None, s, t, p)
    total = sweep(19, 20, total, None, None, t, p)
    total = sweep(20, 21, total, None, None, None, p)

    for copy in copies + thirds:
        copy.wait_recv()

    whole, rim = ((0, 18),), ((0, 2), (16, 18))
    inner, inner_rim = ((1, 17),), ((1, 3), (15, 17))

    def rest_of_first(i, carry):
        rims = [(jnp.minimum(4 + 5 * i + j, CX + 1), rim) for j in range(5)]
        first_rows([(1 + i, whole), (CX + 2 + i, whole), *rims])
        return carry

    def rest_of_second(i, carry):
        rims = [(5 + 4 * i + j, rim) for j in range(4)]
        second_rows([(2 + i, whole), (CX + 1 + i, whole), *rims])
        return carry

    def rest_of_third(i):
        rims = [(jnp.minimum(6 + 4 * i + j, CX - 1), inner_rim) for j in range(4)]
        third_rows([(3 + i, inner), (CX + i, inner), *rims])

    def rest_of_products(i, total):
        total = products(3 + i, inner, total)
        total = products(CX + i, inner, total)
        for j in range(3):
            total = products(6 + 3 * i + j, inner_rim, total)
        return total

    def rest_of_both(i, total):
        total = rest_of_products(i - 1, total)
        rest_of_third(i)
        return total

    lax.fori_loop(0, REACH, rest_of_first, 0)
    lax.fori_loop(0, REACH, rest_of_second, 0)
    rest_of_third(0)
    total = lax.fori_loop(1, REACH, rest_of_both, total)
    total = rest_of_products(REACH - 1, total)
    total = products(CX - 1, inner_rim, total)
    store = pltpu.make_async_copy(split, cols, local_sem.at[2])
    store.start()
    mixed = total[:, COLS:]
    total = total[:, :COLS] + (mixed + mixed.T)
    empty = jnp.zeros((COLS // 2, HALF - COLS), f32)
    total = jnp.concatenate([total[: COLS // 2], empty, total[COLS // 2 :], empty], axis=1)

    for kind, (size, part) in enumerate(zip(GROUPS, (part0, part1, part2))):
        me = place(kind, gx, gy)
        part[me] = total
        sums = []
        for step in range(1, size):
            copy = pltpu.make_async_remote_copy(
                src_ref=part.at[me],
                dst_ref=part.at[me],
                send_sem=sum_send.at[kind, step],
                recv_sem=sum_recv.at[kind, size - step],
                device_id=partner(kind, gx, gy, step),
                device_id_type=MESH,
            )
            copy.start()
            sums.append(copy)
        for copy in sums:
            copy.wait()
        total = part[0]
        for i in range(1, size):
            total = total + part[i]
    gram[...] = total

    for copy in cond_copies + copies + thirds:
        copy.wait_send()
    store.wait()


def basis_kernel(cols, gram, basis, triangle, held, result, load_sem, store_sem):
    f32 = jnp.float32

    def load(x):
        return pltpu.make_async_copy(cols.at[x], held.at[x], load_sem.at[x])

    def begin(x, carry):
        load(x).start()
        return carry

    lax.fori_loop(0, CX, begin, 0)

    packed = gram[...]
    full = jnp.concatenate([packed, pltpu.roll(packed, HALF, 1)], axis=0)
    row = lax.broadcasted_iota(jnp.int32, (8, LANES), 0)
    lane = lax.broadcasted_iota(jnp.int32, (8, LANES), 1)
    count = COLS // 8
    matrix = []
    for i in range(count):
        unit = jnp.where(lane == row + (HALF + 8 * i), 1.0, 0.0)
        matrix.append(jnp.where(lane < COLS, full[8 * i : 8 * i + 8], unit))
    pivots = [jnp.ones((8, LANES), f32) for _ in range(count)]

    def across(v, k):
        return jnp.broadcast_to(v[:, k : k + 1], (8, LANES))

    def down(v, r):
        return jnp.broadcast_to(v[r : r + 1, :], (8, LANES))

    for k in range(0, COLS, 2):
        block, r = k // 8, k % 8
        near = {i: across(matrix[i], k) for i in range(block, count)}
        far = {i: across(matrix[i], k + 1) for i in range(block, count)}
        row_near = down(matrix[block], r)
        row_far = down(matrix[block], r + 1)
        p, q, o = down(near[block], r), down(far[block], r + 1), down(far[block], r)
        inverse_near = 1.0 / p
        inverse_far = p / (p * q - o * o)
        ratio = o * inverse_near
        row_far = row_far - ratio * row_near
        for i in range(block, count):
            first = near[i] * inverse_near
            second = (far[i] - first * o) * inverse_far
            if i == block:
                second = jnp.where(row > r + 1, second, 0.0)
                pivots[i] = jnp.where(row == r, p, pivots[i])
                pivots[i] = jnp.where(row == r + 1, q - ratio * o, pivots[i])
                first = jnp.where(row > r, first, 0.0)
            matrix[i] = matrix[i] - (first * row_near + second * row_far)
    size = math.sqrt(GX * CX * GY * MERGED)
    matrix = jnp.concatenate([m * lax.rsqrt(p) for m, p in zip(matrix, pivots)], axis=0)
    row = lax.broadcasted_iota(jnp.int32, (COLS, LANES), 0)
    lane = lax.broadcasted_iota(jnp.int32, (COLS, LANES), 1)
    upper = jnp.where((lane >= row) & (lane < COLS), matrix * (1.0 / size), 0.0)
    triangle[...] = upper[:, :COLS]
    inverse = pltpu.roll(matrix, HALF, 1)[:, :COLS] * size
    coarse = inverse.astype(jnp.bfloat16)
    fine = (inverse - coarse.astype(f32)).astype(jnp.bfloat16)
    weights = jnp.concatenate([coarse, coarse, fine], axis=1)

    def send(x):
        return pltpu.make_async_copy(result.at[x], basis.at[:, x, :], store_sem.at[x])

    def solve(x, carry):
        load(x).wait()
        both = held[x]
        stack = jnp.concatenate([both, both[:COLS]], axis=0)
        result[x] = jnp.dot(weights, stack, preferred_element_type=f32)
        send(x).start()
        return carry

    lax.fori_loop(0, CX, solve, 0)

    def finish(x, carry):
        send(x).wait()
        return carry

    lax.fori_loop(0, CX, finish, 0)


def per_device(initial_guess, conductivity, electrodes):
    f32 = jnp.float32
    any_space = pl.BlockSpec(memory_space=pltpu.HBM)
    vmem = pl.BlockSpec(memory_space=pltpu.VMEM)
    smem = pl.BlockSpec(memory_space=pltpu.SMEM)
    dma = pltpu.SemaphoreType.DMA
    cols, gram = pl.pallas_call(
        krylov_kernel,
        out_shape=(
            jax.ShapeDtypeStruct((CX, 2 * COLS, MERGED), jnp.bfloat16),
            jax.ShapeDtypeStruct((COLS // 2, LANES), f32),
        ),
        in_specs=[any_space, any_space, smem],
        out_specs=(any_space, vmem),
        scratch_shapes=[
            pltpu.VMEM((EXT_X, SRC, EXT), f32),
            pltpu.VMEM((EXT_X, SRC, EXT), f32),
            pltpu.VMEM((EXT_X, SRC, EXT), f32),
            pltpu.VMEM((CX, SRC, EXT), f32),
            pltpu.VMEM((CX + 16, EXT + 2 * LANES), f32),
            pltpu.VMEM((EXT_T, (CX + 16) * 8, LANES), f32),
            pltpu.VMEM((2 * LANES, 2 * LANES), jnp.bfloat16),
            pltpu.VMEM((2, 4, MERGED), f32),
            pltpu.VMEM((2, 4, MERGED), f32),
            pltpu.VMEM((2, CX // 2, SRC, LANES), f32),
            pltpu.VMEM((2, CX // 2, SRC, LANES), f32),
            pltpu.VMEM((CX, 2 * COLS, MERGED), jnp.bfloat16),
            pltpu.VMEM((GROUPS[0], COLS // 2, LANES), f32),
            pltpu.VMEM((GROUPS[1], COLS // 2, LANES), f32),
            pltpu.VMEM((GROUPS[2], COLS // 2, LANES), f32),
            dma((CX,)),
            dma((3,)),
            dma((8,)),
            dma((8,)),
            dma((8,)),
            dma((8,)),
            dma((2,)),
            dma((2,)),
            dma((3, 8)),
            dma((3, 8)),
        ],
        compiler_params=pltpu.CompilerParams(
            collective_id=0, has_side_effects=True, vmem_limit_bytes=60 * 2**20
        ),
        name="krylov",
    )(initial_guess, conductivity, electrodes)
    basis, triangle = pl.pallas_call(
        basis_kernel,
        out_shape=(
            jax.ShapeDtypeStruct((COLS, CX, MERGED), f32),
            jax.ShapeDtypeStruct((COLS, COLS), f32),
        ),
        in_specs=[any_space, vmem],
        out_specs=(any_space, vmem),
        scratch_shapes=[
            pltpu.VMEM((CX, 2 * COLS, MERGED), jnp.bfloat16),
            pltpu.VMEM((CX, COLS, MERGED), f32),
            dma((CX,)),
            dma((CX,)),
        ],
        compiler_params=pltpu.CompilerParams(vmem_limit_bytes=60 * 2**20),
        name="basis",
    )(cols, gram)
    return basis, triangle


def solution(mesh):
    return jax.shard_map(
        per_device,
        mesh=mesh,
        in_specs=(P(None, "gx", "gy"), P("gx", "gy"), P()),
        out_specs=(P(None, "gx", "gy"), P()),
        check_vma=False,
    )
```

```python
import functools
import math

import jax
import jax.numpy as jnp
from jax import lax
from jax.experimental import pallas as pl
from jax.experimental.pallas import tpu as pltpu
from jax.sharding import PartitionSpec as P

MESH = pl.DeviceIdType.MESH
NZ = 64
SHARE = 2
LANES = 128
HALF = 64
SRC = 16
COLS = 48
CX = 16
TILES = 16
REACH = 3
EXT_X = CX + 2 * REACH
EXT_T = TILES + 2
EXT = EXT_T * LANES
MERGED = TILES * LANES
GX, GY = 32, 8
MOVES = ((1, 0), (-1, 0), (0, 1), (0, -1), (1, 1), (1, -1), (-1, 1), (-1, -1))


def tile(t):
    if isinstance(t, int):
        return pl.ds(t * LANES, LANES)
    return pl.ds(pl.multiple_of(t * LANES, LANES), LANES)


def swap_halves(v):
    return pltpu.roll(v, HALF, 1)


def partner(kind, gx, gy, step):
    if kind == 0:
        base = (gx // 8) * 8
        return (base + lax.rem(gx - base + step, 8), gy)
    if kind == 1:
        return (lax.rem(gx + 8 * step, GX), gy)
    return (gx, lax.rem(gy + step, GY))


def place(kind, gx, gy):
    return (lax.rem(gx, 8), gx // 8, gy)[kind]


GROUPS = (8, 4, 8)


def krylov_kernel(
    guess,
    cond,
    electrodes,
    cols,
    gram,
    start,
    field,
    field_s,
    field_t,
    cond_ext,
    coef,
    shifts,
    cond_out,
    cond_in,
    third_out,
    third_in,
    split,
    part0,
    part1,
    part2,
    guess_sem,
    local_sem,
    cond_send,
    cond_recv,
    send,
    recv,
    third_send_sem,
    third_recv_sem,
    sum_send,
    sum_recv,
):
    gx, gy = lax.axis_index("gx"), lax.axis_index("gy")
    f32 = jnp.float32

    def beside(move):
        dx, dy = move
        return (lax.rem(gx + dx + GX, GX), lax.rem(gy + dy + GY, GY))

    barrier = pltpu.get_barrier_semaphore()
    for move in MOVES:
        pl.semaphore_signal(barrier, inc=1, device_id=beside(move), device_id_type=MESH)

    def load(x):
        return pltpu.make_async_copy(
            guess.at[:, x, :], start.at[REACH + x, :, pl.ds(LANES, MERGED)], guess_sem.at[x]
        )

    faces = (*range(REACH), *range(CX - REACH, CX))
    between = tuple(range(REACH, CX - REACH))
    load_cond = pltpu.make_async_copy(
        cond, cond_ext.at[pl.ds(8, CX), pl.ds(2 * LANES, MERGED)], local_sem.at[1]
    )
    load_cond.start()
    for x in faces + between:
        load(x).start()
    for kind, size in enumerate(GROUPS):
        for step in range(1, size):
            pl.semaphore_signal(
                barrier, inc=1, device_id=partner(kind, gx, gy, step), device_id_type=MESH
            )

    for x in (0, EXT_X - 1):
        for t in (0, EXT_T - 1):
            start[x, :, tile(t)] = jnp.zeros((SRC, LANES), f32)
    for x in (0, 8 + CX):
        for t in (0, EXT_T + 1):
            cond_ext[pl.ds(x, 8), tile(t)] = jnp.zeros((8, LANES), f32)
        cond_ext[pl.ds(x, 8), pl.ds(2 * LANES, MERGED)] = jnp.zeros((8, MERGED), f32)
    load_cond.wait()
    for i, x in enumerate((8 + CX - 4, 8)):
        cond_out[i] = cond_ext[pl.ds(x, 4), pl.ds(2 * LANES, MERGED)]

    pl.semaphore_wait(barrier, len(MOVES) + sum(GROUPS) - len(GROUPS))

    cond_copies = []
    for i, (dx, dy) in enumerate(MOVES):
        if dx == 0:
            rows_from, rows_to = pl.ds(0, CX), pl.ds(8, CX)
        elif dx > 0:
            rows_from, rows_to = pl.ds(CX - 8, 8), pl.ds(0, 8)
        else:
            rows_from, rows_to = pl.ds(0, 8), pl.ds(8 + CX, 8)
        if dy == 0:
            lanes_from = lanes_to = pl.ds(0, MERGED)
        elif dx == 0:
            lanes_from = pl.ds(MERGED - 2 * LANES if dy > 0 else 0, 2 * LANES)
            lanes_to = pl.ds(0 if dy > 0 else (TILES + 2) * LANES, 2 * LANES)
        else:
            lanes_from = tile(TILES - 1 if dy > 0 else 0)
            lanes_to = tile(1 if dy > 0 else TILES + 2)
        source, target = cond.at[rows_from, lanes_from], cond_ext.at[rows_to, lanes_to]
        if dy == 0:
            side = 0 if dx > 0 else 1
            source, target = cond_out.at[side], cond_in.at[side]
        cond_copies.append(
            pltpu.make_async_remote_copy(
                src_ref=source,
                dst_ref=target,
                send_sem=cond_send.at[i],
                recv_sem=cond_recv.at[i],
                device_id=beside((dx, dy)),
                device_id_type=MESH,
            )
        )
    for copy in cond_copies:
        copy.start()

    for x in faces:
        load(x).wait()

    copies = []
    for i, (dx, dy) in enumerate(MOVES):
        depth = REACH if dy == 0 else 2
        if dx == 0:
            x_from, x_to = pl.ds(REACH, CX), pl.ds(REACH, CX)
        elif dx > 0:
            x_from, x_to = pl.ds(REACH + CX - depth, depth), pl.ds(REACH - depth, depth)
        else:
            x_from, x_to = pl.ds(REACH, depth), pl.ds(REACH + CX, depth)
        if dy == 0:
            lanes_from = lanes_to = pl.ds(LANES, MERGED)
        else:
            lanes_from = tile(TILES if dy > 0 else 1)
            lanes_to = tile(0 if dy > 0 else TILES + 1)
        copies.append(
            pltpu.make_async_remote_copy(
                src_ref=start.at[x_from, :, lanes_from],
                dst_ref=start.at[x_to, :, lanes_to],
                send_sem=send.at[i],
                recv_sem=recv.at[i],
                device_id=beside((dx, dy)),
                device_id_type=MESH,
            )
        )
    thirds = [
        pltpu.make_async_remote_copy(
            src_ref=third_out.at[i],
            dst_ref=third_in.at[i],
            send_sem=third_send_sem.at[i],
            recv_sem=third_recv_sem.at[i],
            device_id=beside(move),
            device_id_type=MESH,
        )
        for i, move in enumerate(((0, 1), (0, -1)))
    ]
    along_x = [copy for copy, (dx, dy) in zip(copies, MOVES) if dx != 0]
    along_y = [copy for copy, (dx, dy) in zip(copies, MOVES) if dx == 0]
    for copy in along_x:
        copy.start()

    for x in between:
        load(x).wait()
    lane = lax.broadcasted_iota(jnp.int32, (SRC, LANES), 1)
    low = lane < HALF

    def pack_third(x, carry):
        near, far = REACH + x, REACH + CX // 2 + x
        third_out[0, x] = jnp.where(
            low, swap_halves(start[near, :, tile(TILES - 1)]), start[far, :, tile(TILES - 1)]
        )
        third_out[1, x] = jnp.where(
            low, start[far, :, tile(2)], swap_halves(start[near, :, tile(2)])
        )
        return carry

    lax.fori_loop(0, CX // 2, pack_third, 0)

    for copy in along_y + thirds:
        copy.start()

    for copy in cond_copies:
        copy.wait_recv()
    for i, x in enumerate((4, 8 + CX)):
        outside = (gx == 0, gx == GX - 1)[i]
        cond_ext[pl.ds(x, 4), pl.ds(2 * LANES, MERGED)] = jnp.where(outside, 0.0, cond_in[i])
    row = lax.broadcasted_iota(jnp.int32, (CX + 16, LANES), 0)
    lane_c = lax.broadcasted_iota(jnp.int32, (CX + 16, LANES), 1)
    first_x, last_x = gx == 0, gx == GX - 1
    row_from = jnp.where(first_x, 8, 0)
    row_to = jnp.where(last_x, 8 + CX, 16 + CX)
    for t in (0, 1, TILES + 2, TILES + 3):
        outside = gy == 0 if t < 2 else gy == GY - 1
        kept = (row >= row_from) & (row < jnp.where(outside, 0, row_to))
        cond_ext[:, tile(t)] = jnp.where(kept, cond_ext[:, tile(t)], 0.0)
    z = lax.rem(lane_c, HALF)
    low_c = lane_c < HALF

    def couplings(t, carry):
        here = -0.5 * cond_ext[:, tile(t + 1)]
        below, above = -0.5 * cond_ext[:, tile(t)], -0.5 * cond_ext[:, tile(t + 2)]
        swapped = swap_halves(here)
        outer = jnp.where(low_c, swap_halves(below), swap_halves(above))
        z_down = jnp.where(z == 0, 0.0, pltpu.roll(here, 1, 1))
        z_up = jnp.where(z == HALF - 1, 0.0, pltpu.roll(here, LANES - 1, 1))
        x_down = pltpu.roll(here, 1, 0)
        x_up = pltpu.roll(here, CX + 15, 0)
        total = 6.0 * here
        for k, there in enumerate((x_down, x_up, swapped, outer, z_down, z_up)):
            total = total + there
            face = jnp.where(here * there > 0.0, here + there, 0.0)
            coef[t, pl.ds(k, CX + 16, stride=8), :] = face
        coef[t, pl.ds(6, CX + 16, stride=8), :] = jnp.where(here < 0.0, -total, 0.0)
        return carry

    lax.fori_loop(0, EXT_T, couplings, 0)

    inward = lax.rem(lax.broadcasted_iota(jnp.int32, (2 * LANES, 2 * LANES), 0), LANES)
    outward = lax.broadcasted_iota(jnp.int32, (2 * LANES, 2 * LANES), 1)
    outward = jnp.where(outward < LANES, outward - 1, outward - (LANES - 1))
    shifts[...] = jnp.where(inward == outward, 1.0, 0.0).astype(jnp.bfloat16)

    def along_z(values):
        values = jnp.concatenate(values, axis=0)
        coarse = values.astype(jnp.bfloat16)
        fine = (values - coarse.astype(f32)).astype(jnp.bfloat16)
        both = jnp.concatenate([coarse, fine], axis=1)
        return jnp.dot(both, shifts[...], preferred_element_type=f32)

    def around(read, jobs):
        places = [
            (x, t)
            for x, runs in jobs
            for begin, end in runs
            for t in range(begin, end)
            if t % SHARE == 1
        ]
        both = along_z([read(x, t) for x, t in places])
        found = []
        for x, runs in jobs:
            row = {}
            for begin, end in runs:
                for t in range(begin, end):
                    if t % SHARE == 1:
                        row[t] = both[:SRC, :LANES], both[:SRC, LANES:]
                        both = both[SRC:]
            found.append(row)
        return found

    def stencil(read, x, runs, left, right, shift, emit, beside_z, closed=False):
        base = pl.multiple_of((x + 8 - REACH) * 8, 8)
        for begin, end in runs:
            value = read(x, begin)
            turned = swap_halves(value)
            if closed:
                before = turned
            elif begin > 0:
                before = swap_halves(read(x, begin - 1))
            else:
                before = turned if left is None else left
            for t in range(begin, end):
                c = [
                    jnp.broadcast_to(coef[t, pl.ds(base + k, 1), :], (SRC, LANES))
                    for k in range(7)
                ]
                if closed and t == end - 1:
                    following, after = None, turned
                elif t == EXT_T - 1:
                    following, after = None, turned if right is None else right
                else:
                    following = read(x, t + 1)
                    after = swap_halves(following)
                diagonal = c[6] if shift == 0.0 else c[6] - shift
                if t in beside_z:
                    z_down, z_up = beside_z[t]
                else:
                    z_down, z_up = pltpu.roll(value, 1, 1), pltpu.roll(value, LANES - 1, 1)
                near = diagonal * value + c[2] * turned
                across = c[0] * read(x - 1, t) + c[1] * read(x + 1, t)
                along = c[4] * z_down + c[5] * z_up
                total = (near + across) + (along + c[3] * jnp.where(low, before, after))
                emit(t, total)
                value, before, turned = following, turned, after

    spot = jnp.zeros((SRC, LANES), jnp.int32)
    source = lax.broadcasted_iota(jnp.int32, (SRC, LANES), 0)
    for k in range(SRC):
        spot = jnp.where(source == k, electrodes[k], spot)
    spot = spot - lane

    def outer_thirds(x):
        p = x - REACH
        centre = (p >= 0) & (p < CX)
        held = jnp.where(centre, lax.rem(p + CX // 2, CX // 2), 0)
        far = p >= CX // 2
        left = third_in[0, held]
        right = third_in[1, held]
        left = jnp.where(far, swap_halves(left), left)
        right = jnp.where(far, swap_halves(right), right)
        return left, right

    def read_start(x, t):
        return start[x, :, tile(t)]

    def first_rows(jobs):
        for (x, runs), beside_z in zip(jobs, around(read_start, jobs)):
            first_row(x, runs, beside_z)

    def first_row(x, runs, beside_z):
        cell_x = gx * CX + x - REACH
        inside = (cell_x >= 0) & (cell_x < GX * CX)
        origin = (cell_x * (GY * TILES) + gy * TILES - 1) * LANES
        left = right = None
        if runs[0][0] == 0:
            left, right = outer_thirds(x)

        def emit(t, total):
            ok = inside
            if t == 0:
                ok = ok & (gy > 0)
            if t == EXT_T - 1:
                ok = ok & (gy < GY - 1)
            cell = jnp.where(ok, origin + t * LANES, -(2**30))
            field[x, :, tile(t)] = jnp.where(spot == cell, 20.0, 0.0) - total

        closed = runs[0][0] == 1
        stencil(read_start, x, runs, left, right, 0.0, emit, beside_z, closed)


    def read_first(x, t):
        return field[x, :, tile(t)]

    def second_rows(jobs):
        for (x, runs), beside_z in zip(jobs, around(read_first, jobs)):
            second_row(x, runs, beside_z)

    def second_row(x, runs, beside_z):
        def emit(t, total):
            field_s[x, :, tile(t)] = total

        stencil(read_first, x, runs, None, None, 0.8, emit, beside_z)

    def read_second(x, t):
        return field_s[x, :, tile(t)]

    def third_rows(jobs):
        for (x, runs), beside_z in zip(jobs, around(read_second, jobs)):
            third_row(x, runs, beside_z)

    def third_row(x, runs, beside_z):
        def emit(t, total):
            field_t[x - REACH, :, tile(t)] = total

        stencil(read_second, x, runs, None, None, 1.6, emit, beside_z)

    def products(x, runs, total):
        pieces = []
        for begin, end in runs:
            inner = pl.ds(begin * LANES, (end - begin) * LANES)
            values = jnp.concatenate(
                [field[x, :, inner], field_s[x, :, inner], field_t[x - REACH, :, inner]], axis=0
            )
            coarse = values.astype(jnp.bfloat16)
            fine = (values - coarse.astype(f32)).astype(jnp.bfloat16)
            both = jnp.concatenate([coarse, fine], axis=0)
            split[x - REACH, :, pl.ds((begin - 1) * LANES, (end - begin) * LANES)] = both
            pieces.append(both)
        both = pieces[0] if len(pieces) == 1 else jnp.concatenate(pieces, axis=1)
        return total + lax.dot_general(
            both[:COLS], both, (((1,), (1,)), ((), ())), preferred_element_type=f32
        )

    def sweep(begin, end, total, first=None, second=None, third=None, inner=None):
        def step(x, total):
            if inner:
                total = products(x - 5, inner, total)
            if third:
                third_rows([(x - 4, third)])
            if second:
                second_rows([(x - 2, second)])
            if first:
                first_rows([(x, first)])
            return total

        return lax.fori_loop(begin, end, step, total)

    total = jnp.zeros((COLS, 2 * COLS), f32)
    f, s, t, p = ((1, 17),), ((2, 16),), ((3, 15),), ((3, 15),)
    sweep(4, 7, 0, f)
    sweep(7, 10, 0, f, s)
    sweep(10, 11, 0, f, s, t)
    total = sweep(11, 18, total, f, s, t, p)
    total = sweep(18, 19, total, None, s, t, p)
    total = sweep(19, 20, total, None, None, t, p)
    total = sweep(20, 21, total, None, None, None, p)

    for copy in copies + thirds:
        copy.wait_recv()

    whole, rim = ((0, 18),), ((0, 2), (16, 18))
    inner, inner_rim = ((1, 17),), ((1, 3), (15, 17))

    def rest_of_first(i, carry):
        rims = [(jnp.minimum(4 + 5 * i + j, CX + 1), rim) for j in range(5)]
        first_rows([(1 + i, whole), (CX + 2 + i, whole), *rims])
        return carry

    def rest_of_second(i, carry):
        rims = [(5 + 4 * i + j, rim) for j in range(4)]
        second_rows([(2 + i, whole), (CX + 1 + i, whole), *rims])
        return carry

    def rest_of_third(i):
        rims = [(jnp.minimum(6 + 4 * i + j, CX - 1), inner_rim) for j in range(4)]
        third_rows([(3 + i, inner), (CX + i, inner), *rims])

    def rest_of_products(i, total):
        total = products(3 + i, inner, total)
        total = products(CX + i, inner, total)
        for j in range(3):
            total = products(6 + 3 * i + j, inner_rim, total)
        return total

    def rest_of_both(i, total):
        total = rest_of_products(i - 1, total)
        rest_of_third(i)
        return total

    lax.fori_loop(0, REACH, rest_of_first, 0)
    lax.fori_loop(0, REACH, rest_of_second, 0)
    rest_of_third(0)
    total = lax.fori_loop(1, REACH, rest_of_both, total)
    total = rest_of_products(REACH - 1, total)
    total = products(CX - 1, inner_rim, total)
    store = pltpu.make_async_copy(split, cols, local_sem.at[2])
    store.start()
    mixed = total[:, COLS:]
    total = total[:, :COLS] + (mixed + mixed.T)
    empty = jnp.zeros((COLS // 2, HALF - COLS), f32)
    total = jnp.concatenate([total[: COLS // 2], empty, total[COLS // 2 :], empty], axis=1)

    for kind, (size, part) in enumerate(zip(GROUPS, (part0, part1, part2))):
        me = place(kind, gx, gy)
        part[me] = total
        sums = []
        for step in range(1, size):
            copy = pltpu.make_async_remote_copy(
                src_ref=part.at[me],
                dst_ref=part.at[me],
                send_sem=sum_send.at[kind, step],
                recv_sem=sum_recv.at[kind, size - step],
                device_id=partner(kind, gx, gy, step),
                device_id_type=MESH,
            )
            copy.start()
            sums.append(copy)
        for copy in sums:
            copy.wait()
        total = part[0]
        for i in range(1, size):
            total = total + part[i]
    gram[...] = total

    for copy in cond_copies + copies + thirds:
        copy.wait_send()
    store.wait()


def basis_kernel(cols, gram, basis, triangle, held, result, load_sem, store_sem):
    f32 = jnp.float32
    chunks = 8
    width = MERGED // chunks

    def part(i):
        lanes = pl.ds(pl.multiple_of(i * width, width), width)
        return pltpu.make_async_copy(cols.at[:, :, lanes], held.at[:, :, lanes], load_sem.at[i])

    def begin(i, carry):
        part(i).start()
        return carry

    lax.fori_loop(0, chunks, begin, 0)

    packed = gram[...]
    full = jnp.concatenate([packed, pltpu.roll(packed, HALF, 1)], axis=0)
    row = lax.broadcasted_iota(jnp.int32, (8, LANES), 0)
    lane = lax.broadcasted_iota(jnp.int32, (8, LANES), 1)
    count = COLS // 8
    matrix = []
    for i in range(count):
        unit = jnp.where(lane == row + (HALF + 8 * i), 1.0, 0.0)
        matrix.append(jnp.where(lane < COLS, full[8 * i : 8 * i + 8], unit))
    pivots = [jnp.ones((8, LANES), f32) for _ in range(count)]

    def across(v, k):
        return jnp.broadcast_to(v[:, k : k + 1], (8, LANES))

    def down(v, r):
        return jnp.broadcast_to(v[r : r + 1, :], (8, LANES))

    for k in range(0, COLS, 2):
        block, r = k // 8, k % 8
        near = {i: across(matrix[i], k) for i in range(block, count)}
        far = {i: across(matrix[i], k + 1) for i in range(block, count)}
        row_near = down(matrix[block], r)
        row_far = down(matrix[block], r + 1)
        p, q, o = down(near[block], r), down(far[block], r + 1), down(far[block], r)
        inverse_near = 1.0 / p
        inverse_far = p / (p * q - o * o)
        ratio = o * inverse_near
        row_far = row_far - ratio * row_near
        for i in range(block, count):
            first = near[i] * inverse_near
            second = (far[i] - first * o) * inverse_far
            if i == block:
                second = jnp.where(row > r + 1, second, 0.0)
                pivots[i] = jnp.where(row == r, p, pivots[i])
                pivots[i] = jnp.where(row == r + 1, q - ratio * o, pivots[i])
                first = jnp.where(row > r, first, 0.0)
            matrix[i] = matrix[i] - (first * row_near + second * row_far)
    size = math.sqrt(GX * CX * GY * MERGED)
    matrix = jnp.concatenate([m * lax.rsqrt(p) for m, p in zip(matrix, pivots)], axis=0)
    row = lax.broadcasted_iota(jnp.int32, (COLS, LANES), 0)
    lane = lax.broadcasted_iota(jnp.int32, (COLS, LANES), 1)
    upper = jnp.where((lane >= row) & (lane < COLS), matrix * (1.0 / size), 0.0)
    triangle[...] = upper[:, :COLS]
    inverse = pltpu.roll(matrix, HALF, 1)[:, :COLS] * size
    coarse = inverse.astype(jnp.bfloat16)
    fine = (inverse - coarse.astype(f32)).astype(jnp.bfloat16)
    weights = jnp.concatenate([coarse, coarse, fine], axis=1)

    per_chunk = width // LANES

    def send(h, t):
        return pltpu.make_async_copy(
            result.at[h, t].reshape(COLS, 8, LANES), basis.at[:, h, :, tile(t)], store_sem.at[h, t]
        )

    def solve(i, carry):
        part(i).wait()
        lanes = pl.ds(pl.multiple_of(i * width, width), width)
        for x in range(CX):
            both = held[x, :, lanes]
            stack = jnp.concatenate([both, both[:COLS]], axis=0)
            solved = jnp.dot(weights, stack, preferred_element_type=f32)
            for t in range(per_chunk):
                result[x // 8, i * per_chunk + t, pl.ds(x % 8, COLS, stride=8), :] = solved[
                    :, t * LANES : (t + 1) * LANES
                ]
        for h in range(2):
            for t in range(per_chunk):
                send(h, i * per_chunk + t).start()
        return carry

    lax.fori_loop(0, chunks, solve, 0)

    def finish(t, carry):
        for h in range(2):
            send(h, t).wait()
        return carry

    lax.fori_loop(0, TILES, finish, 0)


def per_device(initial_guess, conductivity, electrodes):
    f32 = jnp.float32
    any_space = pl.BlockSpec(memory_space=pltpu.HBM)
    vmem = pl.BlockSpec(memory_space=pltpu.VMEM)
    smem = pl.BlockSpec(memory_space=pltpu.SMEM)
    dma = pltpu.SemaphoreType.DMA
    cols, gram = pl.pallas_call(
        krylov_kernel,
        out_shape=(
            jax.ShapeDtypeStruct((CX, 2 * COLS, MERGED), jnp.bfloat16),
            jax.ShapeDtypeStruct((COLS // 2, LANES), f32),
        ),
        in_specs=[any_space, any_space, smem],
        out_specs=(any_space, vmem),
        scratch_shapes=[
            pltpu.VMEM((EXT_X, SRC, EXT), f32),
            pltpu.VMEM((EXT_X, SRC, EXT), f32),
            pltpu.VMEM((EXT_X, SRC, EXT), f32),
            pltpu.VMEM((CX, SRC, EXT), f32),
            pltpu.VMEM((CX + 16, EXT + 2 * LANES), f32),
            pltpu.VMEM((EXT_T, (CX + 16) * 8, LANES), f32),
            pltpu.VMEM((2 * LANES, 2 * LANES), jnp.bfloat16),
            pltpu.VMEM((2, 4, MERGED), f32),
            pltpu.VMEM((2, 4, MERGED), f32),
            pltpu.VMEM((2, CX // 2, SRC, LANES), f32),
            pltpu.VMEM((2, CX // 2, SRC, LANES), f32),
            pltpu.VMEM((CX, 2 * COLS, MERGED), jnp.bfloat16),
            pltpu.VMEM((GROUPS[0], COLS // 2, LANES), f32),
            pltpu.VMEM((GROUPS[1], COLS // 2, LANES), f32),
            pltpu.VMEM((GROUPS[2], COLS // 2, LANES), f32),
            dma((CX,)),
            dma((3,)),
            dma((8,)),
            dma((8,)),
            dma((8,)),
            dma((8,)),
            dma((2,)),
            dma((2,)),
            dma((3, 8)),
            dma((3, 8)),
        ],
        compiler_params=pltpu.CompilerParams(
            collective_id=0, has_side_effects=True, vmem_limit_bytes=60 * 2**20
        ),
        name="krylov",
    )(initial_guess, conductivity, electrodes)
    basis, triangle = pl.pallas_call(
        basis_kernel,
        out_shape=(
            jax.ShapeDtypeStruct((COLS, 2, 8, MERGED), f32),
            jax.ShapeDtypeStruct((COLS, COLS), f32),
        ),
        in_specs=[any_space, vmem],
        out_specs=(any_space, vmem),
        scratch_shapes=[
            pltpu.VMEM((CX, 2 * COLS, MERGED), jnp.bfloat16),
            pltpu.VMEM((2, TILES, COLS * 8, LANES), f32),
            dma((8,)),
            dma((2, TILES)),
        ],
        compiler_params=pltpu.CompilerParams(vmem_limit_bytes=60 * 2**20),
        name="basis",
    )(cols, gram)
    return basis.reshape(COLS, CX, MERGED), triangle


def solution(mesh):
    return jax.shard_map(
        per_device,
        mesh=mesh,
        in_specs=(P(None, "gx", "gy"), P("gx", "gy"), P()),
        out_specs=(P(None, "gx", "gy"), P()),
        check_vma=False,
    )
```

```python
import functools
import math

import jax
import jax.numpy as jnp
from jax import lax
from jax.experimental import pallas as pl
from jax.experimental.pallas import tpu as pltpu
from jax.sharding import PartitionSpec as P

MESH = pl.DeviceIdType.MESH
NZ = 64
SHARE = 2
LANES = 128
HALF = 64
SRC = 16
COLS = 48
CX = 16
TILES = 16
REACH = 3
EXT_X = CX + 2 * REACH
EXT_T = TILES + 2
EXT = EXT_T * LANES
MERGED = TILES * LANES
GX, GY = 32, 8
MOVES = ((1, 0), (-1, 0), (0, 1), (0, -1), (1, 1), (1, -1), (-1, 1), (-1, -1))


def tile(t):
    if isinstance(t, int):
        return pl.ds(t * LANES, LANES)
    return pl.ds(pl.multiple_of(t * LANES, LANES), LANES)


def swap_halves(v):
    return pltpu.roll(v, HALF, 1)


def partner(kind, gx, gy, step):
    if kind == 0:
        base = (gx // 8) * 8
        return (base + lax.rem(gx - base + step, 8), gy)
    if kind == 1:
        return (lax.rem(gx + 8 * step, GX), gy)
    return (gx, lax.rem(gy + step, GY))


def place(kind, gx, gy):
    return (lax.rem(gx, 8), gx // 8, gy)[kind]


GROUPS = (8, 4, 8)


def krylov_kernel(
    guess,
    cond,
    electrodes,
    cols,
    gram,
    start,
    field,
    field_s,
    field_t,
    cond_ext,
    coef,
    shifts,
    cond_out,
    cond_in,
    third_out,
    third_in,
    split,
    part0,
    part1,
    part2,
    guess_sem,
    local_sem,
    cond_send,
    cond_recv,
    send,
    recv,
    third_send_sem,
    third_recv_sem,
    sum_send,
    sum_recv,
):
    gx, gy = lax.axis_index("gx"), lax.axis_index("gy")
    f32 = jnp.float32

    def beside(move):
        dx, dy = move
        return (lax.rem(gx + dx + GX, GX), lax.rem(gy + dy + GY, GY))

    barrier = pltpu.get_barrier_semaphore()
    for move in MOVES:
        pl.semaphore_signal(barrier, inc=1, device_id=beside(move), device_id_type=MESH)

    def load(x):
        return pltpu.make_async_copy(
            guess.at[:, x, :], start.at[REACH + x, :, pl.ds(LANES, MERGED)], guess_sem.at[x]
        )

    faces = (*range(REACH), *range(CX - REACH, CX))
    between = tuple(range(REACH, CX - REACH))
    load_cond = pltpu.make_async_copy(
        cond, cond_ext.at[pl.ds(8, CX), pl.ds(2 * LANES, MERGED)], local_sem.at[1]
    )
    load_cond.start()
    for x in faces + between:
        load(x).start()
    for kind, size in enumerate(GROUPS):
        for step in range(1, size):
            pl.semaphore_signal(
                barrier, inc=1, device_id=partner(kind, gx, gy, step), device_id_type=MESH
            )

    for x in (0, EXT_X - 1):
        for t in (0, EXT_T - 1):
            start[x, :, tile(t)] = jnp.zeros((SRC, LANES), f32)
    for x in (0, 8 + CX):
        for t in (0, EXT_T + 1):
            cond_ext[pl.ds(x, 8), tile(t)] = jnp.zeros((8, LANES), f32)
        cond_ext[pl.ds(x, 8), pl.ds(2 * LANES, MERGED)] = jnp.zeros((8, MERGED), f32)
    load_cond.wait()
    for i, x in enumerate((8 + CX - 4, 8)):
        cond_out[i] = cond_ext[pl.ds(x, 4), pl.ds(2 * LANES, MERGED)]

    pl.semaphore_wait(barrier, len(MOVES) + sum(GROUPS) - len(GROUPS))

    cond_copies = []
    for i, (dx, dy) in enumerate(MOVES):
        if dx == 0:
            rows_from, rows_to = pl.ds(0, CX), pl.ds(8, CX)
        elif dx > 0:
            rows_from, rows_to = pl.ds(CX - 8, 8), pl.ds(0, 8)
        else:
            rows_from, rows_to = pl.ds(0, 8), pl.ds(8 + CX, 8)
        if dy == 0:
            lanes_from = lanes_to = pl.ds(0, MERGED)
        elif dx == 0:
            lanes_from = pl.ds(MERGED - 2 * LANES if dy > 0 else 0, 2 * LANES)
            lanes_to = pl.ds(0 if dy > 0 else (TILES + 2) * LANES, 2 * LANES)
        else:
            lanes_from = tile(TILES - 1 if dy > 0 else 0)
            lanes_to = tile(1 if dy > 0 else TILES + 2)
        source, target = cond.at[rows_from, lanes_from], cond_ext.at[rows_to, lanes_to]
        if dy == 0:
            side = 0 if dx > 0 else 1
            source, target = cond_out.at[side], cond_in.at[side]
        cond_copies.append(
            pltpu.make_async_remote_copy(
                src_ref=source,
                dst_ref=target,
                send_sem=cond_send.at[i],
                recv_sem=cond_recv.at[i],
                device_id=beside((dx, dy)),
                device_id_type=MESH,
            )
        )
    for copy in cond_copies:
        copy.start()

    for x in faces:
        load(x).wait()

    copies = []
    for i, (dx, dy) in enumerate(MOVES):
        depth = REACH if dy == 0 else 2
        if dx == 0:
            x_from, x_to = pl.ds(REACH, CX), pl.ds(REACH, CX)
        elif dx > 0:
            x_from, x_to = pl.ds(REACH + CX - depth, depth), pl.ds(REACH - depth, depth)
        else:
            x_from, x_to = pl.ds(REACH, depth), pl.ds(REACH + CX, depth)
        if dy == 0:
            lanes_from = lanes_to = pl.ds(LANES, MERGED)
        else:
            lanes_from = tile(TILES if dy > 0 else 1)
            lanes_to = tile(0 if dy > 0 else TILES + 1)
        copies.append(
            pltpu.make_async_remote_copy(
                src_ref=start.at[x_from, :, lanes_from],
                dst_ref=start.at[x_to, :, lanes_to],
                send_sem=send.at[i],
                recv_sem=recv.at[i],
                device_id=beside((dx, dy)),
                device_id_type=MESH,
            )
        )
    thirds = [
        pltpu.make_async_remote_copy(
            src_ref=third_out.at[i],
            dst_ref=third_in.at[i],
            send_sem=third_send_sem.at[i],
            recv_sem=third_recv_sem.at[i],
            device_id=beside(move),
            device_id_type=MESH,
        )
        for i, move in enumerate(((0, 1), (0, -1)))
    ]
    along_x = [copy for copy, (dx, dy) in zip(copies, MOVES) if dx != 0]
    along_y = [copy for copy, (dx, dy) in zip(copies, MOVES) if dx == 0]
    for copy in along_x:
        copy.start()

    for x in between:
        load(x).wait()
    lane = lax.broadcasted_iota(jnp.int32, (SRC, LANES), 1)
    low = lane < HALF

    def pack_third(x, carry):
        near, far = REACH + x, REACH + CX // 2 + x
        third_out[0, x] = jnp.where(
            low, swap_halves(start[near, :, tile(TILES - 1)]), start[far, :, tile(TILES - 1)]
        )
        third_out[1, x] = jnp.where(
            low, start[far, :, tile(2)], swap_halves(start[near, :, tile(2)])
        )
        return carry

    lax.fori_loop(0, CX // 2, pack_third, 0)

    for copy in along_y + thirds:
        copy.start()

    for copy in cond_copies:
        copy.wait_recv()
    for i, x in enumerate((4, 8 + CX)):
        outside = (gx == 0, gx == GX - 1)[i]
        cond_ext[pl.ds(x, 4), pl.ds(2 * LANES, MERGED)] = jnp.where(outside, 0.0, cond_in[i])
    row = lax.broadcasted_iota(jnp.int32, (CX + 16, LANES), 0)
    lane_c = lax.broadcasted_iota(jnp.int32, (CX + 16, LANES), 1)
    first_x, last_x = gx == 0, gx == GX - 1
    row_from = jnp.where(first_x, 8, 0)
    row_to = jnp.where(last_x, 8 + CX, 16 + CX)
    for t in (0, 1, TILES + 2, TILES + 3):
        outside = gy == 0 if t < 2 else gy == GY - 1
        kept = (row >= row_from) & (row < jnp.where(outside, 0, row_to))
        cond_ext[:, tile(t)] = jnp.where(kept, cond_ext[:, tile(t)], 0.0)
    z = lax.rem(lane_c, HALF)
    low_c = lane_c < HALF

    def couplings(t, carry):
        here = -0.5 * cond_ext[:, tile(t + 1)]
        below, above = -0.5 * cond_ext[:, tile(t)], -0.5 * cond_ext[:, tile(t + 2)]
        swapped = swap_halves(here)
        outer = jnp.where(low_c, swap_halves(below), swap_halves(above))
        z_down = jnp.where(z == 0, 0.0, pltpu.roll(here, 1, 1))
        z_up = jnp.where(z == HALF - 1, 0.0, pltpu.roll(here, LANES - 1, 1))
        x_down = pltpu.roll(here, 1, 0)
        x_up = pltpu.roll(here, CX + 15, 0)
        total = 6.0 * here
        for k, there in enumerate((x_down, x_up, swapped, outer, z_down, z_up)):
            total = total + there
            face = jnp.where(here * there > 0.0, here + there, 0.0)
            coef[t, pl.ds(k, CX + 16, stride=8), :] = face
        coef[t, pl.ds(6, CX + 16, stride=8), :] = jnp.where(here < 0.0, -total, 0.0)
        return carry

    lax.fori_loop(0, EXT_T, couplings, 0)

    inward = lax.rem(lax.broadcasted_iota(jnp.int32, (2 * LANES, 2 * LANES), 0), LANES)
    outward = lax.broadcasted_iota(jnp.int32, (2 * LANES, 2 * LANES), 1)
    outward = jnp.where(outward < LANES, outward - 1, outward - (LANES - 1))
    shifts[...] = jnp.where(inward == outward, 1.0, 0.0).astype(jnp.bfloat16)

    def along_z(values):
        values = jnp.concatenate(values, axis=0)
        coarse = values.astype(jnp.bfloat16)
        fine = (values - coarse.astype(f32)).astype(jnp.bfloat16)
        both = jnp.concatenate([coarse, fine], axis=1)
        return jnp.dot(both, shifts[...], preferred_element_type=f32)

    def around(read, jobs):
        places = [
            (x, t)
            for x, runs in jobs
            for begin, end in runs
            for t in range(begin, end)
            if t % SHARE == 1
        ]
        both = along_z([read(x, t) for x, t in places])
        found = []
        for x, runs in jobs:
            row = {}
            for begin, end in runs:
                for t in range(begin, end):
                    if t % SHARE == 1:
                        row[t] = both[:SRC, :LANES], both[:SRC, LANES:]
                        both = both[SRC:]
            found.append(row)
        return found

    def stencil(read, x, runs, left, right, shift, emit, beside_z, closed=False):
        base = pl.multiple_of((x + 8 - REACH) * 8, 8)
        for begin, end in runs:
            value = read(x, begin)
            turned = swap_halves(value)
            if closed:
                before = turned
            elif begin > 0:
                before = swap_halves(read(x, begin - 1))
            else:
                before = turned if left is None else left
            for t in range(begin, end):
                c = [
                    jnp.broadcast_to(coef[t, pl.ds(base + k, 1), :], (SRC, LANES))
                    for k in range(7)
                ]
                if closed and t == end - 1:
                    following, after = None, turned
                elif t == EXT_T - 1:
                    following, after = None, turned if right is None else right
                else:
                    following = read(x, t + 1)
                    after = swap_halves(following)
                diagonal = c[6] if shift == 0.0 else c[6] - shift
                if t in beside_z:
                    z_down, z_up = beside_z[t]
                else:
                    z_down, z_up = pltpu.roll(value, 1, 1), pltpu.roll(value, LANES - 1, 1)
                near = diagonal * value + c[2] * turned
                across = c[0] * read(x - 1, t) + c[1] * read(x + 1, t)
                along = c[4] * z_down + c[5] * z_up
                total = (near + across) + (along + c[3] * jnp.where(low, before, after))
                emit(t, total)
                value, before, turned = following, turned, after

    spot = jnp.zeros((SRC, LANES), jnp.int32)
    source = lax.broadcasted_iota(jnp.int32, (SRC, LANES), 0)
    for k in range(SRC):
        spot = jnp.where(source == k, electrodes[k], spot)
    spot = spot - lane

    def outer_thirds(x):
        p = x - REACH
        centre = (p >= 0) & (p < CX)
        held = jnp.where(centre, lax.rem(p + CX // 2, CX // 2), 0)
        far = p >= CX // 2
        left = third_in[0, held]
        right = third_in[1, held]
        left = jnp.where(far, swap_halves(left), left)
        right = jnp.where(far, swap_halves(right), right)
        return left, right

    def read_start(x, t):
        return start[x, :, tile(t)]

    def first_rows(jobs):
        for (x, runs), beside_z in zip(jobs, around(read_start, jobs)):
            first_row(x, runs, beside_z)

    def first_row(x, runs, beside_z):
        cell_x = gx * CX + x - REACH
        inside = (cell_x >= 0) & (cell_x < GX * CX)
        origin = (cell_x * (GY * TILES) + gy * TILES - 1) * LANES
        left = right = None
        if runs[0][0] == 0:
            left, right = outer_thirds(x)

        def emit(t, total):
            ok = inside
            if t == 0:
                ok = ok & (gy > 0)
            if t == EXT_T - 1:
                ok = ok & (gy < GY - 1)
            cell = jnp.where(ok, origin + t * LANES, -(2**30))
            field[x, :, tile(t)] = jnp.where(spot == cell, 20.0, 0.0) - total

        closed = runs[0][0] == 1
        stencil(read_start, x, runs, left, right, 0.0, emit, beside_z, closed)


    def read_first(x, t):
        return field[x, :, tile(t)]

    def second_rows(jobs):
        for (x, runs), beside_z in zip(jobs, around(read_first, jobs)):
            second_row(x, runs, beside_z)

    def second_row(x, runs, beside_z):
        def emit(t, total):
            field_s[x, :, tile(t)] = total

        stencil(read_first, x, runs, None, None, 0.8, emit, beside_z)

    def read_second(x, t):
        return field_s[x, :, tile(t)]

    def third_rows(jobs):
        for (x, runs), beside_z in zip(jobs, around(read_second, jobs)):
            third_row(x, runs, beside_z)

    def third_row(x, runs, beside_z):
        def emit(t, total):
            field_t[x - REACH, :, tile(t)] = total

        stencil(read_second, x, runs, None, None, 1.6, emit, beside_z)

    def products(x, runs, total):
        pieces = []
        for begin, end in runs:
            inner = pl.ds(begin * LANES, (end - begin) * LANES)
            values = jnp.concatenate(
                [field[x, :, inner], field_s[x, :, inner], field_t[x - REACH, :, inner]], axis=0
            )
            coarse = values.astype(jnp.bfloat16)
            fine = (values - coarse.astype(f32)).astype(jnp.bfloat16)
            both = jnp.concatenate([coarse, fine], axis=0)
            split[x - REACH, :, pl.ds((begin - 1) * LANES, (end - begin) * LANES)] = both
            pieces.append(both)
        both = pieces[0] if len(pieces) == 1 else jnp.concatenate(pieces, axis=1)
        return total + lax.dot_general(
            both[:COLS], both, (((1,), (1,)), ((), ())), preferred_element_type=f32
        )

    def sweep(begin, end, total, first=None, second=None, third=None, inner=None):
        def step(x, total):
            if inner:
                total = products(x - 5, inner, total)
            if third:
                third_rows([(x - 4, third)])
            if second:
                second_rows([(x - 2, second)])
            if first:
                first_rows([(x, first)])
            return total

        return lax.fori_loop(begin, end, step, total)

    total = jnp.zeros((COLS, 2 * COLS), f32)
    f, s, t, p = ((1, 17),), ((2, 16),), ((3, 15),), ((3, 15),)
    sweep(4, 7, 0, f)
    sweep(7, 10, 0, f, s)
    sweep(10, 11, 0, f, s, t)
    total = sweep(11, 18, total, f, s, t, p)
    total = sweep(18, 19, total, None, s, t, p)
    total = sweep(19, 20, total, None, None, t, p)
    total = sweep(20, 21, total, None, None, None, p)

    for copy in copies + thirds:
        copy.wait_recv()

    whole, rim = ((0, 18),), ((0, 2), (16, 18))
    inner, inner_rim = ((1, 17),), ((1, 3), (15, 17))

    def rest_of_first(i, carry):
        rims = [(jnp.minimum(4 + 5 * i + j, CX + 1), rim) for j in range(5)]
        first_rows([(1 + i, whole), (CX + 2 + i, whole), *rims])
        return carry

    def rest_of_second(i, carry):
        rims = [(5 + 4 * i + j, rim) for j in range(4)]
        second_rows([(2 + i, whole), (CX + 1 + i, whole), *rims])
        return carry

    def rest_of_third(i):
        rims = [(jnp.minimum(6 + 4 * i + j, CX - 1), inner_rim) for j in range(4)]
        third_rows([(3 + i, inner), (CX + i, inner), *rims])

    def rest_of_products(i, total):
        total = products(3 + i, inner, total)
        total = products(CX + i, inner, total)
        for j in range(3):
            total = products(6 + 3 * i + j, inner_rim, total)
        return total

    def rest_of_both(i, total):
        total = rest_of_products(i - 1, total)
        rest_of_third(i)
        return total

    lax.fori_loop(0, REACH, rest_of_first, 0)
    lax.fori_loop(0, REACH, rest_of_second, 0)
    rest_of_third(0)
    total = lax.fori_loop(1, REACH, rest_of_both, total)
    total = rest_of_products(REACH - 1, total)
    total = products(CX - 1, inner_rim, total)
    store = pltpu.make_async_copy(split, cols, local_sem.at[2])
    store.start()
    mixed = total[:, COLS:]
    total = total[:, :COLS] + (mixed + mixed.T)
    empty = jnp.zeros((COLS // 2, HALF - COLS), f32)
    total = jnp.concatenate([total[: COLS // 2], empty, total[COLS // 2 :], empty], axis=1)

    for kind, (size, part) in enumerate(zip(GROUPS, (part0, part1, part2))):
        me = place(kind, gx, gy)
        part[me] = total
        sums = []
        for step in sorted(range(1, size), key=lambda n: abs(2 * n - size)):
            copy = pltpu.make_async_remote_copy(
                src_ref=part.at[me],
                dst_ref=part.at[me],
                send_sem=sum_send.at[kind, step],
                recv_sem=sum_recv.at[kind, size - step],
                device_id=partner(kind, gx, gy, step),
                device_id_type=MESH,
            )
            copy.start()
            sums.append(copy)
        for copy in sums:
            copy.wait()
        total = part[0]
        for i in range(1, size):
            total = total + part[i]
    gram[...] = total

    for copy in cond_copies + copies + thirds:
        copy.wait_send()
    store.wait()


def basis_kernel(cols, gram, basis, triangle, held, result, load_sem, store_sem):
    f32 = jnp.float32
    chunks = 8
    width = MERGED // chunks

    def part(i):
        lanes = pl.ds(pl.multiple_of(i * width, width), width)
        return pltpu.make_async_copy(cols.at[:, :, lanes], held.at[:, :, lanes], load_sem.at[i])

    def begin(i, carry):
        part(i).start()
        return carry

    lax.fori_loop(0, chunks, begin, 0)

    packed = gram[...]
    full = jnp.concatenate([packed, pltpu.roll(packed, HALF, 1)], axis=0)
    row = lax.broadcasted_iota(jnp.int32, (8, LANES), 0)
    lane = lax.broadcasted_iota(jnp.int32, (8, LANES), 1)
    count = COLS // 8
    matrix = []
    for i in range(count):
        unit = jnp.where(lane == row + (HALF + 8 * i), 1.0, 0.0)
        matrix.append(jnp.where(lane < COLS, full[8 * i : 8 * i + 8], unit))
    pivots = [jnp.ones((8, LANES), f32) for _ in range(count)]

    def across(v, k):
        return jnp.broadcast_to(v[:, k : k + 1], (8, LANES))

    def down(v, r):
        return jnp.broadcast_to(v[r : r + 1, :], (8, LANES))

    for k in range(0, COLS, 2):
        block, r = k // 8, k % 8
        near = {i: across(matrix[i], k) for i in range(block, count)}
        far = {i: across(matrix[i], k + 1) for i in range(block, count)}
        row_near = down(matrix[block], r)
        row_far = down(matrix[block], r + 1)
        p, q, o = down(near[block], r), down(far[block], r + 1), down(far[block], r)
        inverse_near = 1.0 / p
        inverse_far = p / (p * q - o * o)
        ratio = o * inverse_near
        row_far = row_far - ratio * row_near
        for i in range(block, count):
            first = near[i] * inverse_near
            second = (far[i] - first * o) * inverse_far
            if i == block:
                second = jnp.where(row > r + 1, second, 0.0)
                pivots[i] = jnp.where(row == r, p, pivots[i])
                pivots[i] = jnp.where(row == r + 1, q - ratio * o, pivots[i])
                first = jnp.where(row > r, first, 0.0)
            matrix[i] = matrix[i] - (first * row_near + second * row_far)
    size = math.sqrt(GX * CX * GY * MERGED)
    matrix = jnp.concatenate([m * lax.rsqrt(p) for m, p in zip(matrix, pivots)], axis=0)
    row = lax.broadcasted_iota(jnp.int32, (COLS, LANES), 0)
    lane = lax.broadcasted_iota(jnp.int32, (COLS, LANES), 1)
    upper = jnp.where((lane >= row) & (lane < COLS), matrix * (1.0 / size), 0.0)
    triangle[...] = upper[:, :COLS]
    inverse = pltpu.roll(matrix, HALF, 1)[:, :COLS] * size
    coarse = inverse.astype(jnp.bfloat16)
    fine = (inverse - coarse.astype(f32)).astype(jnp.bfloat16)
    weights = jnp.concatenate([coarse, coarse, fine], axis=1)

    per_chunk = width // LANES

    def send(h, t):
        return pltpu.make_async_copy(
            result.at[h, t].reshape(COLS, 8, LANES), basis.at[:, h, :, tile(t)], store_sem.at[h, t]
        )

    def solve(i, carry):
        part(i).wait()
        lanes = pl.ds(pl.multiple_of(i * width, width), width)
        for x in range(CX):
            both = held[x, :, lanes]
            stack = jnp.concatenate([both, both[:COLS]], axis=0)
            solved = jnp.dot(weights, stack, preferred_element_type=f32)
            for t in range(per_chunk):
                result[x // 8, i * per_chunk + t, pl.ds(x % 8, COLS, stride=8), :] = solved[
                    :, t * LANES : (t + 1) * LANES
                ]
        for h in range(2):
            for t in range(per_chunk):
                send(h, i * per_chunk + t).start()
        return carry

    lax.fori_loop(0, chunks, solve, 0)

    def finish(t, carry):
        for h in range(2):
            send(h, t).wait()
        return carry

    lax.fori_loop(0, TILES, finish, 0)


def per_device(initial_guess, conductivity, electrodes):
    f32 = jnp.float32
    any_space = pl.BlockSpec(memory_space=pltpu.HBM)
    vmem = pl.BlockSpec(memory_space=pltpu.VMEM)
    smem = pl.BlockSpec(memory_space=pltpu.SMEM)
    dma = pltpu.SemaphoreType.DMA
    cols, gram = pl.pallas_call(
        krylov_kernel,
        out_shape=(
            jax.ShapeDtypeStruct((CX, 2 * COLS, MERGED), jnp.bfloat16),
            jax.ShapeDtypeStruct((COLS // 2, LANES), f32),
        ),
        in_specs=[any_space, any_space, smem],
        out_specs=(any_space, vmem),
        scratch_shapes=[
            pltpu.VMEM((EXT_X, SRC, EXT), f32),
            pltpu.VMEM((EXT_X, SRC, EXT), f32),
            pltpu.VMEM((EXT_X, SRC, EXT), f32),
            pltpu.VMEM((CX, SRC, EXT), f32),
            pltpu.VMEM((CX + 16, EXT + 2 * LANES), f32),
            pltpu.VMEM((EXT_T, (CX + 16) * 8, LANES), f32),
            pltpu.VMEM((2 * LANES, 2 * LANES), jnp.bfloat16),
            pltpu.VMEM((2, 4, MERGED), f32),
            pltpu.VMEM((2, 4, MERGED), f32),
            pltpu.VMEM((2, CX // 2, SRC, LANES), f32),
            pltpu.VMEM((2, CX // 2, SRC, LANES), f32),
            pltpu.VMEM((CX, 2 * COLS, MERGED), jnp.bfloat16),
            pltpu.VMEM((GROUPS[0], COLS // 2, LANES), f32),
            pltpu.VMEM((GROUPS[1], COLS // 2, LANES), f32),
            pltpu.VMEM((GROUPS[2], COLS // 2, LANES), f32),
            dma((CX,)),
            dma((3,)),
            dma((8,)),
            dma((8,)),
            dma((8,)),
            dma((8,)),
            dma((2,)),
            dma((2,)),
            dma((3, 8)),
            dma((3, 8)),
        ],
        compiler_params=pltpu.CompilerParams(
            collective_id=0, has_side_effects=True, vmem_limit_bytes=60 * 2**20
        ),
        name="krylov",
    )(initial_guess, conductivity, electrodes)
    basis, triangle = pl.pallas_call(
        basis_kernel,
        out_shape=(
            jax.ShapeDtypeStruct((COLS, 2, 8, MERGED), f32),
            jax.ShapeDtypeStruct((COLS, COLS), f32),
        ),
        in_specs=[any_space, vmem],
        out_specs=(any_space, vmem),
        scratch_shapes=[
            pltpu.VMEM((CX, 2 * COLS, MERGED), jnp.bfloat16),
            pltpu.VMEM((2, TILES, COLS * 8, LANES), f32),
            dma((8,)),
            dma((2, TILES)),
        ],
        compiler_params=pltpu.CompilerParams(vmem_limit_bytes=60 * 2**20),
        name="basis",
    )(cols, gram)
    return basis.reshape(COLS, CX, MERGED), triangle


def solution(mesh):
    return jax.shard_map(
        per_device,
        mesh=mesh,
        in_specs=(P(None, "gx", "gy"), P("gx", "gy"), P()),
        out_specs=(P(None, "gx", "gy"), P()),
        check_vma=False,
    )
```
